256 devices in a mesh: tok: 16 (over z, core), voc: 16 (over x, y).
Axes of the slice: x: 4, y: 4, z: 8, core: 2. Of those that a mesh axis runs over, the one named last changes fastest.
Arguments:
- target_logits: bfloat16 [2048, 128256], P('tok', 'voc'), may hold values from -30 to 250
- hidden: bfloat16 [2048, 4096], P('tok', 'voc'), may hold values from -4 to 4
- gain: bfloat16 [4096], P('voc'), may hold values from 0.099609375 to 1.8984375
- head_weight: bfloat16 [4096, 16000], P(None, 'voc'), may hold values from -5 to 5
- draft_ids: int32 [16000], replicated, may hold values from 0 to 128255, as said below
- token_ids: int32 [2048], P('tok'), may hold values from 0 to 128255, as said below
Outputs:
- d_hidden: float32 [2048, 4096], P('tok', 'voc')
- token_loss: float32 [2048], P('tok')
The draws below stay inside these ranges and needn't reach their ends.
Inputs may be any that keep to these rules, and one draw needn't show every extreme that they name: `draft_ids`: the 16000 ids are distinct. Entry i belongs to voc index i // 1000. Of the 1000 ids of one voc index at most 152 lie in one block of 8016 consecutive ids, and for every voc index some block holds exactly 152 of them. `token_ids`: the first token of each block of 128 tokens is one of draft_ids.
All inputs are finite; a program needn't handle non-finite values.
Results may differ from the reference program's by a relative error of at most 0.0058.
Values may be sent and summed in bfloat16 or wider, within the bound.
A program may use at most 64 MiB of HBM per device.

```python
import math
import jax
import jax.numpy as jnp
from jax import lax

H = 4096
VDEV = 8016
DVD = 1000
TOK_DEV = 128
TOKENS = 2048
V = 128256
DV = 16000
CAP = 152


def draft_layout(key):
    shards = V // VDEV
    key_order, key_moves, key_perm, key_shuffle = jax.random.split(key, 4)
    pair_count = (shards - 1) // 2
    even_share = (DVD - CAP) // (shards - 1)
    spare_units = DVD - CAP - even_share * (shards - 1)
    levels = even_share + (jnp.arange(shards - 1, dtype=jnp.int32) < spare_units).astype(jnp.int32)
    moves = jax.random.randint(key_moves, (shards, pair_count), 0, even_share // 2 + 1, dtype=jnp.int32)
    swing = jnp.stack([moves, -moves], axis=2).reshape(shards, 2 * pair_count)
    swing = jnp.pad(swing, ((0, 0), (0, shards - 1 - 2 * pair_count)))
    ranked = jnp.concatenate([jnp.full((shards, 1), CAP, jnp.int32), levels[None, :] + swing], axis=1)
    orders = jax.vmap(lambda sub_key: jax.random.permutation(sub_key, shards))(jax.random.split(key_order, shards))
    placing = (orders[:, :, None] == jnp.arange(shards, dtype=jnp.int32)[None, None, :]).astype(jnp.int32)
    counts = jnp.sum(ranked[:, :, None] * placing, axis=1).astype(jnp.int32)
    offsets = jnp.cumsum(counts, axis=0) - counts
    loads = jnp.sum(counts, axis=0).astype(jnp.int32)
    perms = jax.vmap(lambda sub_key: jax.random.permutation(sub_key, VDEV))(jax.random.split(key_perm, shards)).astype(jnp.int32)
    ends = jnp.cumsum(counts, axis=1)
    positions = jnp.arange(DVD, dtype=jnp.int32)
    which_shard = jnp.sum((positions[None, :, None] >= ends[:, None, :]).astype(jnp.int32), axis=2)
    begins = jnp.take_along_axis(ends - counts, which_shard, axis=1)
    bases = jnp.take_along_axis(offsets, which_shard, axis=1)
    local_ids = perms[which_shard, bases + positions[None, :] - begins]
    owner_ids = which_shard * VDEV + local_ids
    shuffles = jax.vmap(lambda sub_key: jax.random.permutation(sub_key, DVD))(jax.random.split(key_shuffle, shards))
    owner_ids = jnp.take_along_axis(owner_ids, shuffles, axis=1)
    return (owner_ids.reshape(shards * DVD).astype(jnp.int32), perms, loads)


def draw_draft_ids(key, part):
    layout = draft_layout(key)
    return layout[0]


def draw_token_ids(key, part):
    layout = draft_layout(key)
    key = jax.random.fold_in(key, 5)
    draft_list, perms, loads = layout
    shards = V // VDEV
    key_pick, key_draft, key_block, key_spot = jax.random.split(key, 4)
    groups = TOKENS // TOK_DEV
    row_index = jnp.arange(TOKENS, dtype=jnp.int32)
    group_index = row_index // TOK_DEV
    limits = 30 + 60 * group_index // max(groups - 1, 1)
    inside = (jax.random.randint(key_pick, (TOKENS,), 0, 100, dtype=jnp.int32) < limits) | (row_index % TOK_DEV == 0)
    chosen = draft_list[jax.random.randint(key_draft, (TOKENS,), 0, shards * DVD, dtype=jnp.int32)]
    blocks = jax.random.randint(key_block, (TOKENS,), 0, shards, dtype=jnp.int32)
    spots = jax.random.randint(key_spot, (TOKENS,), loads[blocks], VDEV, dtype=jnp.int32)
    outside = blocks * VDEV + perms[blocks, spots]
    return jnp.where(inside, chosen, outside).astype(jnp.int32)


def draw_target_logits(key, part):
    key = jax.random.fold_in(key, 7)
    key_base = jax.random.fold_in(key, 0)
    values = 3.0 * jax.random.truncated_normal(key_base, -6.0, 6.0, (TOKENS, V))
    return values.astype(jnp.float32).astype(jnp.bfloat16)


def draw_hidden(key, part):
    key = jax.random.fold_in(key, 13)
    key_base, key_rows, key_cols = jax.random.split(key, 3)
    row_scale = jnp.exp(jax.random.uniform(key_rows, (TOKENS, 1), minval=math.log(0.03), maxval=math.log(0.3)))
    col_scale = jnp.exp(jax.random.uniform(key_cols, (1, H), minval=math.log(0.3), maxval=math.log(3.0)))
    values = jax.random.truncated_normal(key_base, -4.0, 4.0, (TOKENS, H)) * row_scale * col_scale
    return values.astype(jnp.float32).astype(jnp.bfloat16)


def draw_head_weight(key, part):
    key = jax.random.fold_in(key, 9)
    key_base = jax.random.fold_in(key, 0)
    unit = 1.0 / math.sqrt(H)
    values = jax.random.truncated_normal(key_base, -6.0, 6.0, (H, DV)) * (3.0 * unit)
    return values.astype(jnp.float32).astype(jnp.bfloat16)


def setup_inputs(seed: int = 0) -> dict:
    seeds = jax.random.split(jax.random.key(seed), 7)
    target_logits = draw_target_logits(jax.random.fold_in(seeds[6], 71), 0)
    hidden = draw_hidden(jax.random.fold_in(seeds[6], 71), 0)
    gain = jnp.clip(1.0 + 0.18 * jax.random.normal(seeds[2], (H,), jnp.float32), 0.099609375, 1.8984375).astype(jnp.bfloat16)
    head_weight = draw_head_weight(jax.random.fold_in(seeds[6], 71), 0)
    draft_ids = draw_draft_ids(jax.random.fold_in(seeds[6], 71), 0)
    token_ids = draw_token_ids(jax.random.fold_in(seeds[6], 71), 0)
    return dict(target_logits=target_logits, hidden=hidden, gain=gain, head_weight=head_weight, draft_ids=draft_ids, token_ids=token_ids)


def block_lse(row_block):
    values = row_block.astype(jnp.float32)
    top_value = lax.optimization_barrier(jnp.max(values, axis=1))
    return top_value + jnp.log(lax.optimization_barrier(jnp.sum(jnp.exp(values - top_value[:, None]), axis=1)))

def reference(target_logits, hidden, gain, head_weight, draft_ids, token_ids):
    valid = jnp.any(token_ids[:, None] == draft_ids[None, :], axis=1).astype(jnp.float32)
    weight = valid * (TOKENS / jnp.sum(valid))
    row_blocks = target_logits.reshape(TOKENS // TOK_DEV, TOK_DEV, V)
    target_lse = lax.map(block_lse, row_blocks).reshape(TOKENS)
    picked = jnp.take(target_logits, draft_ids, axis=1).astype(jnp.float32)
    target_probs = jnp.exp(picked - target_lse[:, None])
    hidden_wide = hidden.astype(jnp.float32)
    gain_wide = gain.astype(jnp.float32)
    inv_scale = lax.rsqrt(lax.optimization_barrier(jnp.mean(hidden_wide * hidden_wide, axis=1)) + 1e-05)
    normed = (hidden_wide * inv_scale[:, None] * gain_wide[None, :]).astype(jnp.bfloat16)
    draft_logits = jnp.dot(normed, head_weight, preferred_element_type=jnp.float32)
    top_draft = lax.optimization_barrier(jnp.max(draft_logits, axis=1))
    draft_lse = top_draft + jnp.log(lax.optimization_barrier(jnp.sum(jnp.exp(draft_logits - top_draft[:, None]), axis=1)))
    draft_mass = lax.optimization_barrier(jnp.sum(target_probs, axis=1))
    cross_term = lax.optimization_barrier(jnp.sum(target_probs * draft_logits, axis=1))
    token_loss = weight * (draft_mass * draft_lse - cross_term)
    soft_probs = jnp.exp(draft_logits - draft_lse[:, None])
    grad_logits = (weight[:, None] * (draft_mass[:, None] * soft_probs - target_probs)).astype(jnp.bfloat16)
    grad_normed = lax.dot_general(grad_logits, head_weight, (((1,), (1,)), ((), ())), preferred_element_type=jnp.float32)
    inner = lax.optimization_barrier(jnp.sum(hidden_wide * gain_wide[None, :] * grad_normed, axis=1))
    cubed = inv_scale * inv_scale * inv_scale
    d_hidden = gain_wide[None, :] * inv_scale[:, None] * grad_normed - hidden_wide * (cubed * inner / H)[:, None]
    return (d_hidden, token_loss)
```

```python
import functools
import jax
import jax.numpy as jnp
from jax import lax
from jax.experimental import pallas as pl
from jax.experimental.pallas import tpu as pltpu
from jax.sharding import PartitionSpec as P

epsilon = 1e-05
MESH = pl.DeviceIdType.MESH
f32 = jnp.float32
bf16 = jnp.bfloat16
NT = (((1,), (1,)), ((), ()))


def up(value, unit):
    return -(-value // unit) * unit


def body(
    dims,
    ids_ref,
    tok_ref,
    hid_ref,
    gain_ref,
    x_hbm,
    w_hbm,
    dh_ref,
    loss_ref,
    x_v,
    w_v,
    hall,
    nrm,
    table,
    stage,
    psend,
    precv,
    pwide,
    key_v,
    col_v,
    slot_f,
    slot_v,
    slot_s,
    idx_v,
    idx_s,
    logits,
    lt,
    pt,
    grad_t,
    stats,
    count,
    gsend,
    grecv,
    local_sem,
    h_send,
    h_recv,
    p_send,
    p_recv,
    s_send,
    s_recv,
    c_send,
    c_recv,
    g_send,
    g_recv,
):
    n, m, vd, dv, cap = dims
    rows, part = hid_ref.shape
    width = n * part
    dp = ids_ref.shape[1]
    slots = psend.shape[1]
    i = lax.axis_index("tok")
    j = lax.axis_index("voc")

    copy_x = pltpu.make_async_copy(x_hbm, x_v, local_sem.at[0])
    copy_w = pltpu.make_async_copy(w_hbm, w_v, local_sem.at[1])
    copy_x.start()
    copy_w.start()

    barrier = pltpu.get_barrier_semaphore()

    def greet_voc(step, _):
        peer = lax.rem(j + step, n)
        pl.semaphore_signal(barrier, inc=1, device_id=(i, peer), device_id_type=MESH)
        return 0

    def greet_tok(step, _):
        peer = lax.rem(i + step, m)
        pl.semaphore_signal(barrier, inc=1, device_id=(peer, j), device_id_type=MESH)
        return 0

    lax.fori_loop(1, n, greet_voc, 0)
    lax.fori_loop(1, m, greet_tok, 0)

    hall[j, 0:rows, :] = hid_ref[...]
    hall[j, rows : rows + 16, :] = jnp.broadcast_to(
        gain_ref[...].astype(f32), (16, part)
    ).astype(bf16)

    pl.semaphore_wait(barrier, n + m - 2)

    def h_copy(slot, peer):
        return pltpu.make_async_remote_copy(
            src_ref=hall.at[j],
            dst_ref=hall.at[slot],
            send_sem=h_send.at[peer],
            recv_sem=h_recv.at[slot],
            device_id=(i, peer),
            device_id_type=MESH,
        )

    def h_start(step, _):
        h_copy(j, lax.rem(j + step, n)).start()
        return 0

    lax.fori_loop(1, n, h_start, 0)

    ids = ids_ref[...]
    low = (j * vd).astype(f32)
    mine = (ids >= low) & (ids < low + vd)
    own = ids_ref[pl.ds(j, 1), :]
    home = jnp.zeros_like(own)
    for k in range(1, n):
        home += (own >= float(k * vd)).astype(f32)
    shard_row = lax.broadcasted_iota(jnp.int32, (n, dp), 0).astype(f32)
    hit = (shard_row == home).astype(f32)
    before = (
        lax.broadcasted_iota(jnp.int32, (dp, dp), 0)
        < lax.broadcasted_iota(jnp.int32, (dp, dp), 1)
    ).astype(f32).astype(bf16)
    rank_mine = jnp.dot(mine.astype(f32).astype(bf16), before, preferred_element_type=f32)
    rank_hit = jnp.dot(hit.astype(bf16), before, preferred_element_type=f32)
    rank_own = jnp.sum(rank_hit * hit, axis=0, keepdims=True)
    key_v[...] = jnp.where(mine, rank_mine, -1.0)
    col_v[...] = ids - low
    idx_v[...] = jnp.clip(
        jnp.broadcast_to(home * slots + rank_own, idx_v.shape).astype(jnp.int32), 0, n * slots - 1
    )

    slot_row = lax.broadcasted_iota(jnp.int32, (slots, dp), 0).astype(f32)
    slot_lane = lax.broadcasted_iota(jnp.int32, (slots, 128), 1)

    def slot_step(k, acc):
        keys = key_v[pl.ds(k, 1), :]
        cols = col_v[pl.ds(k, 1), :]
        found = jnp.sum(jnp.where(slot_row == keys, cols, 0.0), axis=1, keepdims=True)
        return jnp.where(slot_lane == k, found, acc)

    slot_f[...] = jnp.zeros_like(slot_f)
    slot_f[0:slots, :] = lax.fori_loop(0, n, slot_step, jnp.zeros((slots, 128), f32))
    slot_v[...] = jnp.clip(slot_f[...].T[0:n, :].astype(jnp.int32), 0, vd - 1)
    copy_slot = pltpu.make_async_copy(slot_v, slot_s, local_sem.at[2])
    copy_idx = pltpu.make_async_copy(idx_v, idx_s, local_sem.at[3])
    copy_slot.start()
    copy_idx.start()

    token_rows = jnp.broadcast_to(tok_ref[...], (rows, rows)).T

    def valid_step(k, acc):
        entries = ids_ref[pl.ds(k, 1), :]
        for c in range(dp // 128):
            acc = jnp.where(entries[:, c * 128 : (c + 1) * 128] == token_rows, 1.0, acc)
        return acc

    valid = lax.fori_loop(0, n, valid_step, jnp.zeros((rows, 128), f32))
    valid = jnp.max(valid.T, axis=0, keepdims=True)
    count[i] = jnp.broadcast_to(jnp.sum(valid, axis=1, keepdims=True), (8, 128))

    def c_copy(slot, peer):
        return pltpu.make_async_remote_copy(
            src_ref=count.at[i],
            dst_ref=count.at[slot],
            send_sem=c_send.at[peer],
            recv_sem=c_recv.at[slot],
            device_id=(peer, j),
            device_id_type=MESH,
        )

    def c_start(step, _):
        c_copy(i, lax.rem(i + step, m)).start()
        return 0

    lax.fori_loop(1, m, c_start, 0)

    copy_x.wait()
    piece = 256
    whole = vd // piece
    tail = vd - whole * piece
    eye = (
        lax.broadcasted_iota(jnp.int32, (piece, piece), 0)
        == lax.broadcasted_iota(jnp.int32, (piece, piece), 1)
    ).astype(f32).astype(bf16)

    def turn(c, _):
        at = pl.multiple_of(c * piece, piece)
        table[pl.ds(at, piece), :] = lax.dot_general(
            eye, x_v[:, pl.ds(at, piece)], NT, preferred_element_type=f32
        )
        return 0

    lax.fori_loop(0, whole, turn, 0)
    if tail:
        table[whole * piece : vd, :] = lax.dot_general(
            eye[0:tail, 0:tail], x_v[:, whole * piece : vd], NT, preferred_element_type=f32
        )

    copy_slot.wait()
    copy_idx.wait()
    stage[...] = jnp.zeros_like(stage)

    def p_copy(slot, peer):
        return pltpu.make_async_remote_copy(
            src_ref=psend.at[peer],
            dst_ref=precv.at[slot],
            send_sem=p_send.at[peer],
            recv_sem=p_recv.at[slot],
            device_id=(i, peer),
            device_id_type=MESH,
        )

    def pick(k):
        def pick_rows(q, _):
            for u in range(8):
                at = q * 8 + u
                entry = jnp.clip(slot_s[k, at], 0, vd - 1)
                stage[pl.ds(at, 1), :] = table[pl.ds(entry, 1), :]
            return 0

        lax.fori_loop(0, cap // 8, pick_rows, 0)
        return stage[...].astype(bf16)

    def pick_step(step, _):
        peer = lax.rem(j + step, n)
        psend[peer] = pick(peer)
        p_copy(j, peer).start()
        return 0

    lax.fori_loop(1, n, pick_step, 0)
    precv[j] = pick(j)

    parts = 6
    span = vd // parts
    top_target = lax.fori_loop(
        0,
        parts,
        lambda c, top: jnp.maximum(
            top, jnp.max(table[pl.ds(pl.multiple_of(c * span, 8), span), :], axis=0, keepdims=True)
        ),
        jnp.full((1, rows), -1e30, f32),
    )
    total_target = lax.fori_loop(
        0,
        parts,
        lambda c, total: total
        + jnp.sum(
            jnp.exp(table[pl.ds(pl.multiple_of(c * span, 8), span), :] - top_target),
            axis=0,
            keepdims=True,
        ),
        jnp.zeros((1, rows), f32),
    )

    def h_wait(step, _):
        h_copy(lax.rem(j + step, n), j).wait_recv()
        return 0

    lax.fori_loop(1, n, h_wait, 0)

    def square(k, acc):
        wide = hall[k, 0:rows, :].astype(f32)
        return acc + wide * wide

    squares = lax.fori_loop(0, n, square, jnp.zeros((rows, part), f32))
    inv = lax.rsqrt(jnp.sum(squares, axis=1, keepdims=True) / width + epsilon)

    def normalise(k, _):
        wide = hall[k, 0:rows, :].astype(f32)
        gains = hall[k, rows : rows + 16, :].astype(f32)[0:1, :]
        at = pl.multiple_of(k * part, part)
        nrm[:, pl.ds(at, part)] = (wide * inv * gains).astype(bf16)
        return 0

    lax.fori_loop(0, n, normalise, 0)
    inv_row = jnp.broadcast_to(inv, (rows, 128)).T[0:1, :]

    copy_w.wait()
    logits[:, 0:dv] = jnp.dot(nrm[...], w_v[...], preferred_element_type=f32)
    lt[...] = logits[...].T
    draft = lt[0:dv, :]
    top_draft = jnp.max(draft, axis=0, keepdims=True)
    lifted = jnp.exp(draft - top_draft)
    total_draft = jnp.sum(lifted, axis=0, keepdims=True)
    cross_draft = jnp.sum(lifted * draft, axis=0, keepdims=True)

    def p_wait(step, _):
        p_copy(lax.rem(j + step, n), j).wait_recv()
        return 0

    lax.fori_loop(1, n, p_wait, 0)

    def widen(k, _):
        pwide[pl.ds(pl.multiple_of(k * slots, 8), slots), :] = precv[k].astype(f32)
        return 0

    lax.fori_loop(0, n, widen, 0)

    def place(q, _):
        for u in range(8):
            at = q * 8 + u
            entry = jnp.clip(idx_s[0, at], 0, n * slots - 1)
            pt[pl.ds(at, 1), :] = pwide[pl.ds(entry, 1), :]
        return 0

    lax.fori_loop(0, dv // 8, place, 0)
    picked = pt[...]
    top_picked = jnp.max(picked, axis=0, keepdims=True)
    raised = jnp.exp(picked - top_picked)
    total_picked = jnp.sum(raised, axis=0, keepdims=True)
    cross_picked = jnp.sum(raised * lt[0:dv, :], axis=0, keepdims=True)

    tops = (top_target, top_picked, top_picked, top_draft, top_draft)
    sums = (total_target, total_picked, cross_picked, total_draft, cross_draft)
    stats[j] = jnp.zeros((16, 128), f32)
    for r in range(5):
        stats[j, r : r + 1, :] = tops[r]
        stats[j, 8 + r : 9 + r, :] = sums[r]

    def s_copy(slot, peer):
        return pltpu.make_async_remote_copy(
            src_ref=stats.at[j],
            dst_ref=stats.at[slot],
            send_sem=s_send.at[peer],
            recv_sem=s_recv.at[slot],
            device_id=(i, peer),
            device_id_type=MESH,
        )

    def s_start(step, _):
        s_copy(j, lax.rem(j + step, n)).start()
        return 0

    def s_wait(step, _):
        s_copy(lax.rem(j + step, n), j).wait_recv()
        return 0

    def c_wait(step, _):
        c_copy(lax.rem(i + step, m), i).wait_recv()
        return 0

    lax.fori_loop(1, n, s_start, 0)
    lax.fori_loop(1, m, c_wait, 0)
    valid_total = jnp.sum(count[...], axis=0)[0:1, :]
    weight = valid * (float(rows * m) / valid_total)
    hid_t = hid_ref[...].astype(f32).T
    gain_t = jnp.broadcast_to(gain_ref[...].astype(f32), (rows, part)).T
    lax.fori_loop(1, n, s_wait, 0)

    top = stats[0, 0:8, :]
    for k in range(1, n):
        top = jnp.maximum(top, stats[k, 0:8, :])
    total = jnp.zeros((8, 128), f32)
    for k in range(n):
        total += stats[k, 8:16, :] * jnp.exp(stats[k, 0:8, :] - top)
    target_lse = top[0:1, :] + jnp.log(total[0:1, :])
    factor = jnp.exp(top[1:2, :] - target_lse)
    mass = total[1:2, :] * factor
    cross = total[2:3, :] * factor
    draft_lse = top[3:4, :] + jnp.log(total[3:4, :])
    loss_ref[...] = weight * (mass * draft_lse - cross)
    spread = weight * (mass * (total[4:5, :] / total[3:4, :]) - cross)
    shrink = inv_row * inv_row * spread / width

    soft = jnp.exp(lt[0:dv, :] - draft_lse)
    probs = jnp.exp(pt[...] - target_lse)
    grad_t[...] = (weight * (mass * soft - probs)).astype(bf16)

    def g_copy(slot, peer):
        return pltpu.make_async_remote_copy(
            src_ref=gsend.at[peer],
            dst_ref=grecv.at[slot],
            send_sem=g_send.at[peer],
            recv_sem=g_recv.at[slot],
            device_id=(i, peer),
            device_id_type=MESH,
        )

    def term(k):
        at = pl.multiple_of(k * part, part)
        return jnp.dot(w_v[pl.ds(at, part), :], grad_t[...], preferred_element_type=f32)

    def g_step(step, _):
        peer = lax.rem(j + step, n)
        gsend[peer] = term(peer).astype(bf16)
        g_copy(j, peer).start()
        return 0

    lax.fori_loop(1, n, g_step, 0)

    def g_sum(step, acc):
        slot = lax.rem(j + step, n)
        g_copy(slot, j).wait_recv()
        return acc + grecv[slot].astype(f32)

    grad_normed = lax.fori_loop(1, n, g_sum, term(j))
    dh_ref[...] = (gain_t * inv_row * grad_normed - hid_t * shrink).T

    def finish_voc(step, _):
        peer = lax.rem(j + step, n)
        h_copy(j, peer).wait_send()
        p_copy(j, peer).wait_send()
        s_copy(j, peer).wait_send()
        g_copy(j, peer).wait_send()
        return 0

    def finish_tok(step, _):
        c_copy(i, lax.rem(i + step, m)).wait_send()
        return 0

    lax.fori_loop(1, n, finish_voc, 0)
    lax.fori_loop(1, m, finish_tok, 0)


def per_device(target_logits, hidden, gain, head_weight, draft_ids, token_ids):
    n = lax.axis_size("voc")
    m = lax.axis_size("tok")
    rows, part = hidden.shape
    vd = target_logits.shape[1]
    width, dv = head_weight.shape
    cap = 8 * (5 * dv // (16 * n))
    slots = up(cap, 16)
    dp = up(dv, 128)
    slot_lanes = up(slots, 128)
    ids = jnp.pad(
        draft_ids.reshape(n, dv).astype(f32), ((0, 0), (0, dp - dv)), constant_values=-1.0
    )
    tokens = token_ids.astype(f32).reshape(1, rows)
    vmem = pl.BlockSpec(memory_space=pltpu.VMEM)
    anywhere = pl.BlockSpec(memory_space=pl.ANY)
    dma = pltpu.SemaphoreType.DMA
    d_hidden, loss = pl.pallas_call(
        functools.partial(body, (n, m, vd, dv, cap)),
        out_shape=(
            jax.ShapeDtypeStruct((rows, part), f32),
            jax.ShapeDtypeStruct((1, rows), f32),
        ),
        in_specs=[vmem, vmem, vmem, vmem, anywhere, anywhere],
        out_specs=(vmem, vmem),
        scratch_shapes=[
            pltpu.VMEM((rows, vd), bf16),
            pltpu.VMEM((width, dv), bf16),
            pltpu.VMEM((n, rows + 16, part), bf16),
            pltpu.VMEM((rows, width), bf16),
            pltpu.VMEM((vd, rows), f32),
            pltpu.VMEM((slots, rows), f32),
            pltpu.VMEM((n, slots, rows), bf16),
            pltpu.VMEM((n, slots, rows), bf16),
            pltpu.VMEM((n * slots, rows), f32),
            pltpu.VMEM((n, dp), f32),
            pltpu.VMEM((n, dp), f32),
            pltpu.VMEM((slot_lanes, 128), f32),
            pltpu.VMEM((n, slot_lanes), jnp.int32),
            pltpu.SMEM((n, slot_lanes), jnp.int32),
            pltpu.VMEM((8, dp), jnp.int32),
            pltpu.SMEM((8, dp), jnp.int32),
            pltpu.VMEM((rows, dp), f32),
            pltpu.VMEM((dp, rows), f32),
            pltpu.VMEM((dv, rows), f32),
            pltpu.VMEM((dv, rows), bf16),
            pltpu.VMEM((n, 16, 128), f32),
            pltpu.VMEM((m, 8, 128), f32),
            pltpu.VMEM((n, part, rows), bf16),
            pltpu.VMEM((n, part, rows), bf16),
            dma((4,)),
            dma((n,)),
            dma((n,)),
            dma((n,)),
            dma((n,)),
            dma((n,)),
            dma((n,)),
            dma((m,)),
            dma((m,)),
            dma((n,)),
            dma((n,)),
        ],
        compiler_params=pltpu.CompilerParams(
            collective_id=0, has_side_effects=True, vmem_limit_bytes=48 * 1024 * 1024
        ),
    )(ids, tokens, hidden, gain.reshape(1, part), target_logits, head_weight)
    return d_hidden, loss.reshape(rows)


def solution(mesh):
    in_specs = (P("tok", "voc"), P("tok", "voc"), P("voc"), P(None, "voc"), P(), P("tok"))
    out_specs = (P("tok", "voc"), P("tok"))
    return jax.shard_map(
        per_device, mesh=mesh, in_specs=in_specs, out_specs=out_specs, check_vma=False
    )
```

```python
import functools
import math
import jax
import jax.numpy as jnp
from jax import lax
from jax.experimental import pallas as pl
from jax.experimental.pallas import tpu as pltpu
from jax.sharding import PartitionSpec as P

epsilon = 1e-05
MESH = pl.DeviceIdType.MESH
f32 = jnp.float32
bf16 = jnp.bfloat16
NT = (((1,), (1,)), ((), ()))


def up(value, unit):
    return -(-value // unit) * unit


def body(
    dims,
    ids_hbm,
    tok_hbm,
    gain_hbm,
    hid_hbm,
    x_hbm,
    w_hbm,
    dh_ref,
    loss_ref,
    ids_v,
    tok_v,
    gain_v,
    x_v,
    w_v,
    hall,
    nrm,
    table,
    stage,
    psend,
    precv,
    pwide,
    idm_v,
    key_v,
    col_v,
    slot_f,
    slot_v,
    slot_s,
    idx_v,
    idx_s,
    lt,
    pt,
    wide_grad,
    grad,
    stat_x,
    stat_y,
    count_out,
    count_in,
    gsend,
    own_a,
    own_b,
    g1a,
    g1b,
    send_a,
    send_b,
    g2a,
    g2b,
    local_sem,
    entered,
    ha_first,
    hb_first,
    ha_next,
    hb_next,
    ha_recv,
    hb_recv,
    p_send,
    p_recv,
    sx_send,
    sx_recv,
    sy_send,
    sy_recv,
    c_send,
    c_recv,
    ga_send,
    gb_send,
    g1a_recv,
    g1b_recv,
    g2a_send,
    g2b_send,
    g2a_recv,
    g2b_recv,
):
    n, m, vd, dv, cap = dims
    side = math.isqrt(n)
    bits = m.bit_length() - 1
    part = hall.shape[2]
    rows = nrm.shape[0]
    half = rows // 2
    width = n * part
    chunks = idx_v.shape[0]
    slots = psend.shape[1]
    i = lax.axis_index("tok")
    j = lax.axis_index("voc")
    x = j // side
    y = lax.rem(j, side)

    def along_x(step):
        return lax.rem(x + step, side)

    def along_y(step):
        return lax.rem(y + step, side)

    def partner(bit):
        return i + (1 - 2 * lax.rem(i // 2**bit, 2)) * 2**bit

    copy_ids = pltpu.make_async_copy(ids_hbm, ids_v, local_sem.at[0])
    copy_hid = pltpu.make_async_copy(hid_hbm, hall.at[j, 0:rows], local_sem.at[1])
    copy_gain = pltpu.make_async_copy(gain_hbm, gain_v, local_sem.at[2])
    copy_tok = pltpu.make_async_copy(tok_hbm, tok_v, local_sem.at[3])
    copy_x = pltpu.make_async_copy(x_hbm, x_v, local_sem.at[4])
    copy_w = pltpu.make_async_copy(w_hbm, w_v, local_sem.at[5])
    copy_ids.start()
    copy_hid.start()
    copy_gain.start()
    copy_tok.start()
    copy_x.start()
    copy_w.start()

    barrier = pltpu.get_barrier_semaphore()

    def greet(step, _):
        for peer in (along_x(step) * side + y, x * side + along_y(step)):
            pl.semaphore_signal(barrier, inc=1, device_id=(i, peer), device_id_type=MESH)
        return 0

    lax.fori_loop(1, side, greet, 0)
    for bit in range(bits):
        pl.semaphore_signal(barrier, inc=1, device_id=(partner(bit), j), device_id_type=MESH)

    copy_ids.wait()
    lane = lax.broadcasted_iota(jnp.int32, (chunks, 128), 1)
    entry = lax.broadcasted_iota(jnp.int32, (chunks, 128), 0) * 128 + lane
    total_rows = ids_v.shape[0]
    for k in range(n):
        first, shift = divmod(k * dv, 128)
        piece = ids_v[first : min(first + chunks + 1, total_rows), :].astype(f32)
        if shift:
            piece = pltpu.roll(piece, 128 - shift, 1)
        if piece.shape[0] == chunks:
            piece = jnp.concatenate([piece, piece[0:1, :]], axis=0)
        early = jnp.where(lane < 128 - shift, piece[0:chunks, :], piece[1 : chunks + 1, :])
        idm_v[k * chunks : (k + 1) * chunks, :] = jnp.where(entry < dv, early, -1.0)
    ids = idm_v[...]
    low = (j * vd).astype(f32)
    mine = ((ids >= low) & (ids < low + vd)).astype(f32)
    own = idm_v[pl.ds(pl.multiple_of(j * chunks, chunks), chunks), :]
    home = jnp.zeros_like(own)
    for k in range(1, n):
        home += (own >= float(k * vd)).astype(f32)
    home_all = jnp.concatenate([home] * n, axis=0)
    tall = (n * chunks, 128)
    row_shard = (lax.broadcasted_iota(jnp.int32, tall, 0) // chunks).astype(f32)
    hit = (home_all == row_shard).astype(f32)
    before = (
        lax.broadcasted_iota(jnp.int32, (128, 128), 0)
        < lax.broadcasted_iota(jnp.int32, (128, 128), 1)
    ).astype(f32).astype(bf16)
    ones = jnp.ones((128, 128), bf16)
    square_rows = (n * chunks, n * chunks)
    at_row = lax.broadcasted_iota(jnp.int32, square_rows, 0)
    at_column = lax.broadcasted_iota(jnp.int32, square_rows, 1)
    earlier = (
        (at_column < at_row) & (at_column >= at_row - at_row % chunks)
    ).astype(f32).astype(bf16)

    def ranks(mask):
        mask = mask.astype(bf16)
        ahead = jnp.dot(earlier, mask, preferred_element_type=f32).astype(bf16)
        return jnp.dot(mask, before, preferred_element_type=f32) + jnp.dot(
            ahead, ones, preferred_element_type=f32
        )

    key_v[...] = jnp.where(mine > 0.5, ranks(mine), -1.0)
    col_v[...] = ids - low
    rank_hit = ranks(hit) * hit
    rank_own = rank_hit[0:chunks, :]
    for k in range(1, n):
        rank_own += rank_hit[k * chunks : (k + 1) * chunks, :]
    idx_v[...] = jnp.clip((home * slots + rank_own).astype(jnp.int32), 0, n * slots - 1)

    copy_hid.wait()
    copy_gain.wait()
    wide_gain = gain_v[...].astype(f32)
    wide_gain = jnp.concatenate([wide_gain[r : r + 1, :] for r in range(part // 128)], axis=1)
    hall[j, rows : rows + 16, :] = jnp.broadcast_to(wide_gain, (16, part)).astype(bf16)

    pl.semaphore_wait(barrier, 2 * (side - 1) + bits)

    def ha_copy(block, to_x, to_y, send_sem):
        piece = hall.at[block, 0:half]
        return pltpu.make_async_remote_copy(
            src_ref=piece,
            dst_ref=piece,
            send_sem=send_sem,
            recv_sem=ha_recv.at[block],
            device_id=(i, to_x * side + to_y),
            device_id_type=MESH,
        )

    def hb_copy(block, to_x, to_y, send_sem):
        piece = hall.at[block, half : rows + 16]
        return pltpu.make_async_remote_copy(
            src_ref=piece,
            dst_ref=piece,
            send_sem=send_sem,
            recv_sem=hb_recv.at[block],
            device_id=(i, to_x * side + to_y),
            device_id_type=MESH,
        )

    def ha_forward(from_x, step):
        to_y = along_y(step)
        return ha_copy(from_x * side + y, x, to_y, ha_next.at[from_x, to_y])

    def hb_forward(from_y, step):
        to_x = along_x(step)
        return hb_copy(x * side + from_y, to_x, y, hb_next.at[from_y, to_x])

    def h_first(step, _):
        ha_copy(j, along_x(step), y, ha_first.at[along_x(step)]).start()
        hb_copy(j, x, along_y(step), hb_first.at[along_y(step)]).start()
        return 0

    def h_own(step, _):
        ha_forward(x, step).start()
        hb_forward(y, step).start()
        pl.semaphore_signal(
            entered, inc=1, device_id=(i, x * side + along_y(step)), device_id_type=MESH
        )
        return 0

    lax.fori_loop(1, side, h_first, 0)
    lax.fori_loop(1, side, h_own, 0)

    slot_row = lax.broadcasted_iota(jnp.int32, (slots, 128), 0).astype(f32)
    slot_lane = lax.broadcasted_iota(jnp.int32, (slots, 128), 1)

    def slot_step(k, acc):
        at = pl.multiple_of(k * chunks, chunks)
        keys = key_v[pl.ds(at, chunks), :]
        cols = col_v[pl.ds(at, chunks), :]
        found = jnp.zeros((slots, 128), f32)
        for c in range(chunks):
            found = jnp.where(slot_row == keys[c : c + 1, :], cols[c : c + 1, :], found)
        return jnp.where(slot_lane == k, jnp.sum(found, axis=1, keepdims=True), acc)

    slot_f[...] = jnp.zeros_like(slot_f)
    slot_f[0:slots, :] = lax.fori_loop(0, n, slot_step, jnp.zeros((slots, 128), f32))
    slot_v[...] = jnp.clip(slot_f[...].T[0:n, :].astype(jnp.int32), 0, vd - 1)
    copy_slot = pltpu.make_async_copy(slot_v, slot_s, local_sem.at[6])
    copy_idx = pltpu.make_async_copy(idx_v, idx_s, local_sem.at[7])
    copy_slot.start()
    copy_idx.start()

    def h_pass(step, _):
        from_x = along_x(step)
        from_y = along_y(step)
        ha_forward(from_x, 1).wait_recv()
        for later in range(1, side):
            ha_forward(from_x, later).start()
        hb_forward(from_y, 1).wait_recv()
        for later in range(1, side):
            hb_forward(from_y, later).start()
        return 0

    lax.fori_loop(1, side, h_pass, 0)

    copy_tok.wait()
    token_rows = jnp.broadcast_to(tok_v[...].astype(f32), (rows, rows)).T

    def valid_step(k, acc):
        entries = idm_v[pl.ds(pl.multiple_of(k * chunks, chunks), chunks), :]
        for c in range(chunks):
            acc = jnp.where(entries[c : c + 1, :] == token_rows, 1.0, acc)
        return acc

    valid = lax.fori_loop(0, n, valid_step, jnp.zeros((rows, 128), f32))
    valid = jnp.max(valid.T, axis=0, keepdims=True)

    def c_copy(bit):
        return pltpu.make_async_remote_copy(
            src_ref=count_out.at[bit],
            dst_ref=count_in.at[bit],
            send_sem=c_send.at[bit],
            recv_sem=c_recv.at[bit],
            device_id=(partner(bit), j),
            device_id_type=MESH,
        )

    def c_start(bit, value):
        count_out[bit] = value
        c_copy(bit).start()

    def c_sum(bit):
        c_copy(bit).wait_recv()
        return count_out[bit] + count_in[bit]

    c_start(0, jnp.broadcast_to(jnp.sum(valid, axis=1, keepdims=True), (8, 128)))

    copy_x.wait()
    parts = 3
    span = vd // parts

    def widen_target(c, top):
        at = pl.multiple_of(c * span, 16)
        wide = x_v[pl.ds(at, span), :].astype(f32)
        table[pl.ds(at, span), :] = wide
        return jnp.maximum(top, jnp.max(wide, axis=0, keepdims=True))

    top_target = lax.fori_loop(0, parts, widen_target, jnp.full((1, rows), -1e30, f32))

    copy_slot.wait()
    copy_idx.wait()
    stage[...] = jnp.zeros_like(stage)

    def p_copy(slot, peer):
        return pltpu.make_async_remote_copy(
            src_ref=psend.at[peer],
            dst_ref=precv.at[slot],
            send_sem=p_send.at[peer],
            recv_sem=p_recv.at[slot],
            device_id=(i, peer),
            device_id_type=MESH,
        )

    def pick(k):
        for at in range(cap):
            stage[at : at + 1, :] = table[pl.ds(slot_s[k, at], 1), :]
        return stage[...].astype(bf16)

    def pick_step(step, _):
        peer = lax.rem(j + step, n)
        psend[peer] = pick(peer)
        p_copy(j, peer).start()
        return 0

    pl.semaphore_wait(entered, side - 1)
    lax.fori_loop(1, n, pick_step, 0)
    precv[j] = pick(j)

    total_target = lax.fori_loop(
        0,
        parts,
        lambda c, total: total
        + jnp.sum(
            jnp.exp(table[pl.ds(pl.multiple_of(c * span, 8), span), :] - top_target),
            axis=0,
            keepdims=True,
        ),
        jnp.zeros((1, rows), f32),
    )
    if bits > 1:
        c_start(1, c_sum(0))

    def h_rest(step, _):
        from_y = along_y(step)

        def h_rest_a(xs, _):
            ha_copy(xs * side + from_y, x, from_y, ha_next.at[0, 0]).wait_recv()
            return 0

        lax.fori_loop(0, side, h_rest_a, 0)
        from_x = along_x(step)

        def h_rest_b(ys, _):
            hb_copy(from_x * side + ys, from_x, y, hb_next.at[0, 0]).wait_recv()
            return 0

        lax.fori_loop(0, side, h_rest_b, 0)
        return 0

    lax.fori_loop(1, side, h_rest, 0)

    def square(k, acc):
        wide = hall[k, 0:rows, :].astype(f32)
        return acc + wide * wide

    squares = lax.fori_loop(0, n, square, jnp.zeros((rows, part), f32))
    inv = lax.rsqrt(jnp.sum(squares, axis=1, keepdims=True) / width + epsilon)

    def normalise(k, _):
        wide = hall[k, 0:rows, :].astype(f32)
        gains = hall[k, rows : rows + 16, :].astype(f32)[0:1, :]
        at = pl.multiple_of(k * part, part)
        nrm[:, pl.ds(at, part)] = (wide * inv * gains).astype(bf16)
        return 0

    lax.fori_loop(0, n, normalise, 0)
    inv_row = jnp.broadcast_to(inv, (rows, 128)).T[0:1, :]
    if bits > 2:
        c_start(2, c_sum(1))

    copy_w.wait()
    lt[...] = lax.dot_general(w_v[...], nrm[...], NT, preferred_element_type=f32)
    draft = lt[...]
    top_draft = jnp.max(draft, axis=0, keepdims=True)
    lifted = jnp.exp(draft - top_draft)
    total_draft = jnp.sum(lifted, axis=0, keepdims=True)
    cross_draft = jnp.sum(lifted * draft, axis=0, keepdims=True)
    if bits > 3:
        c_start(3, c_sum(2))

    def p_wait(step, _):
        p_copy(lax.rem(j + step, n), j).wait_recv()
        return 0

    lax.fori_loop(1, n, p_wait, 0)

    def widen(k, _):
        pwide[pl.ds(pl.multiple_of(k * slots, 8), slots), :] = precv[k].astype(f32)
        return 0

    lax.fori_loop(0, n, widen, 0)
    for at in range(dv):
        pt[at : at + 1, :] = pwide[pl.ds(idx_s[at // 128, at % 128], 1), :]
    picked = pt[...]
    top_picked = jnp.max(picked, axis=0, keepdims=True)
    raised = jnp.exp(picked - top_picked)
    total_picked = jnp.sum(raised, axis=0, keepdims=True)
    cross_picked = jnp.sum(raised * lt[...], axis=0, keepdims=True)

    tops = (top_target, top_picked, top_picked, top_draft, top_draft)
    sums = (total_target, total_picked, cross_picked, total_draft, cross_draft)
    stat_x[x] = jnp.zeros((16, 128), f32)
    for r in range(5):
        stat_x[x, r : r + 1, :] = tops[r]
        stat_x[x, 8 + r : 9 + r, :] = sums[r]

    def sx_copy(slot, to_x):
        return pltpu.make_async_remote_copy(
            src_ref=stat_x.at[slot],
            dst_ref=stat_x.at[slot],
            send_sem=sx_send.at[to_x],
            recv_sem=sx_recv.at[slot],
            device_id=(i, to_x * side + y),
            device_id_type=MESH,
        )

    def sy_copy(slot, to_y):
        return pltpu.make_async_remote_copy(
            src_ref=stat_y.at[slot],
            dst_ref=stat_y.at[slot],
            send_sem=sy_send.at[to_y],
            recv_sem=sy_recv.at[slot],
            device_id=(i, x * side + to_y),
            device_id_type=MESH,
        )

    def merge(ref):
        top = ref[0, 0:8, :]
        for k in range(1, side):
            top = jnp.maximum(top, ref[k, 0:8, :])
        total = jnp.zeros((8, 128), f32)
        for k in range(side):
            total += ref[k, 8:16, :] * jnp.exp(ref[k, 0:8, :] - top)
        return top, total

    for step in range(1, side):
        sx_copy(x, along_x(step)).start()
    valid_total = c_sum(bits - 1)[0:1, :]
    weight = valid * (float(rows * m) / valid_total)
    for step in range(1, side):
        sx_copy(along_x(step), x).wait_recv()
    top, total = merge(stat_x)
    stat_y[y, 0:8, :] = top
    stat_y[y, 8:16, :] = total
    for step in range(1, side):
        sy_copy(y, along_y(step)).start()
    for step in range(1, side):
        sy_copy(along_y(step), y).wait_recv()
    top, total = merge(stat_y)

    target_lse = top[0:1, :] + jnp.log(total[0:1, :])
    factor = jnp.exp(top[1:2, :] - target_lse)
    mass = total[1:2, :] * factor
    cross = total[2:3, :] * factor
    draft_lse = top[3:4, :] + jnp.log(total[3:4, :])
    loss_ref[...] = weight * (mass * draft_lse - cross)
    spread = weight * (mass * (total[4:5, :] / total[3:4, :]) - cross)
    shrink = inv_row * inv_row * spread / width

    soft = jnp.exp(lt[...] - draft_lse)
    probs = jnp.exp(pt[...] - target_lse)
    wide_grad[dv:, :] = jnp.zeros((wide_grad.shape[0] - dv, rows), f32)
    wide_grad[0:dv, :] = weight * (mass * soft - probs)
    grad[...] = wide_grad[...].T.astype(bf16)
    shrink = jnp.broadcast_to(shrink, (rows, rows)).T[:, 0:1]

    def term(to_x, to_y):
        at = pl.multiple_of((to_x * side + to_y) * part, part)
        return jnp.dot(grad[:, 0:dv], w_v[:, pl.ds(at, part)], preferred_element_type=f32)

    def g1a_copy(from_x, to_x, to_y):
        return pltpu.make_async_remote_copy(
            src_ref=gsend.at[to_x, to_y, 0:half],
            dst_ref=g1a.at[from_x, to_y],
            send_sem=ga_send.at[to_x, to_y],
            recv_sem=g1a_recv.at[from_x, to_y],
            device_id=(i, to_x * side + y),
            device_id_type=MESH,
        )

    def g1b_copy(from_y, to_x, to_y):
        return pltpu.make_async_remote_copy(
            src_ref=gsend.at[to_x, to_y, half:rows],
            dst_ref=g1b.at[from_y, to_x],
            send_sem=gb_send.at[to_x, to_y],
            recv_sem=g1b_recv.at[from_y, to_x],
            device_id=(i, x * side + to_y),
            device_id_type=MESH,
        )

    def g_both(t, _):
        to_x = along_x(t // (side - 1) + 1)
        to_y = along_y(t % (side - 1) + 1)
        gsend[to_x, to_y] = term(to_x, to_y).astype(bf16)
        g1a_copy(x, to_x, to_y).start()
        g1b_copy(y, to_x, to_y).start()
        return 0

    def g_column(step, _):
        to_x = along_x(step)
        value = term(to_x, y)
        gsend[to_x, y] = value.astype(bf16)
        g1a_copy(x, to_x, y).start()
        own_b[to_x] = value[half:rows, :]
        return 0

    def g_row(step, _):
        to_y = along_y(step)
        value = term(x, to_y)
        gsend[x, to_y] = value.astype(bf16)
        g1b_copy(y, x, to_y).start()
        own_a[to_y] = value[0:half, :]
        return 0

    lax.fori_loop(0, (side - 1) * (side - 1), g_both, 0)
    lax.fori_loop(1, side, g_column, 0)
    lax.fori_loop(1, side, g_row, 0)
    value = term(x, y)
    own_a[y] = value[0:half, :]
    own_b[x] = value[half:rows, :]

    def sum_a(to_y):
        acc = own_a[to_y]
        for step in range(1, side):
            from_x = along_x(step)
            g1a_copy(from_x, x, to_y).wait_recv()
            acc += g1a[from_x, to_y].astype(f32)
        return acc

    def sum_b(to_x):
        acc = own_b[to_x]
        for step in range(1, side):
            from_y = along_y(step)
            g1b_copy(from_y, to_x, y).wait_recv()
            acc += g1b[from_y, to_x].astype(f32)
        return acc

    def g2a_copy(from_y, to_y):
        return pltpu.make_async_remote_copy(
            src_ref=send_a.at[to_y],
            dst_ref=g2a.at[from_y],
            send_sem=g2a_send.at[to_y],
            recv_sem=g2a_recv.at[from_y],
            device_id=(i, x * side + to_y),
            device_id_type=MESH,
        )

    def g2b_copy(from_x, to_x):
        return pltpu.make_async_remote_copy(
            src_ref=send_b.at[to_x],
            dst_ref=g2b.at[from_x],
            send_sem=g2b_send.at[to_x],
            recv_sem=g2b_recv.at[from_x],
            device_id=(i, to_x * side + y),
            device_id_type=MESH,
        )

    def g_second(step, _):
        to_y = along_y(step)
        send_a[to_y] = sum_a(to_y).astype(bf16)
        g2a_copy(y, to_y).start()
        to_x = along_x(step)
        send_b[to_x] = sum_b(to_x).astype(bf16)
        g2b_copy(x, to_x).start()
        return 0

    lax.fori_loop(1, side, g_second, 0)
    first = sum_a(y)
    second = sum_b(x)
    for step in range(1, side):
        from_y = along_y(step)
        g2a_copy(from_y, y).wait_recv()
        first += g2a[from_y].astype(f32)
        from_x = along_x(step)
        g2b_copy(from_x, x).wait_recv()
        second += g2b[from_x].astype(f32)
    wide_hidden = hall[j, 0:rows, :].astype(f32)
    dh_ref[0:half, :] = (
        wide_gain * inv[0:half, :] * first - wide_hidden[0:half, :] * shrink[0:half, :]
    )
    dh_ref[half:rows, :] = (
        wide_gain * inv[half:rows, :] * second - wide_hidden[half:rows, :] * shrink[half:rows, :]
    )

    def finish_voc(step, _):
        peer = lax.rem(j + step, n)
        p_copy(j, peer).wait_send()
        return 0

    def finish_side(step, _):
        to_x = along_x(step)
        to_y = along_y(step)
        ha_copy(j, to_x, y, ha_first.at[to_x]).wait_send()
        hb_copy(j, x, to_y, hb_first.at[to_y]).wait_send()
        for origin in range(side):
            ha_forward(origin, step).wait_send()
            hb_forward(origin, step).wait_send()
        sx_copy(x, to_x).wait_send()
        sy_copy(y, to_y).wait_send()
        for other in range(side):
            g1a_copy(x, to_x, other).wait_send()
            g1b_copy(y, other, to_y).wait_send()
        g2a_copy(y, to_y).wait_send()
        g2b_copy(x, to_x).wait_send()
        return 0

    lax.fori_loop(1, n, finish_voc, 0)
    lax.fori_loop(1, side, finish_side, 0)
    for bit in range(bits):
        c_copy(bit).wait_send()


def per_device(target_logits, hidden, gain, head_weight, draft_ids, token_ids):
    n = lax.axis_size("voc")
    m = lax.axis_size("tok")
    rows, part = hidden.shape
    vd = target_logits.shape[1]
    width, dv = head_weight.shape
    side = math.isqrt(n)
    half = rows // 2
    cap = 8 * (5 * dv // (16 * n))
    slots = up(cap, 16)
    dp = up(dv, 128)
    chunks = dp // 128
    slot_lanes = up(slots, 128)
    id_rows = n * dv // 128
    bits = m.bit_length() - 1
    vmem = pl.BlockSpec(memory_space=pltpu.VMEM)
    anywhere = pl.BlockSpec(memory_space=pl.ANY)
    dma = pltpu.SemaphoreType.DMA
    d_hidden, loss = pl.pallas_call(
        functools.partial(body, (n, m, vd, dv, cap)),
        out_shape=(
            jax.ShapeDtypeStruct((rows, part), f32),
            jax.ShapeDtypeStruct((1, rows), f32),
        ),
        in_specs=[anywhere] * 6,
        out_specs=(vmem, vmem),
        scratch_shapes=[
            pltpu.VMEM((id_rows, 128), jnp.int32),
            pltpu.VMEM((1, rows), jnp.int32),
            pltpu.VMEM((part // 128, 128), bf16),
            pltpu.VMEM((vd, rows), bf16),
            pltpu.VMEM((dv, width), bf16),
            pltpu.VMEM((n, rows + 16, part), bf16),
            pltpu.VMEM((rows, width), bf16),
            pltpu.VMEM((vd, rows), f32),
            pltpu.VMEM((slots, rows), f32),
            pltpu.VMEM((n, slots, rows), bf16),
            pltpu.VMEM((n, slots, rows), bf16),
            pltpu.VMEM((n * slots, rows), f32),
            pltpu.VMEM((n * chunks, 128), f32),
            pltpu.VMEM((n * chunks, 128), f32),
            pltpu.VMEM((n * chunks, 128), f32),
            pltpu.VMEM((slot_lanes, 128), f32),
            pltpu.VMEM((n, slot_lanes), jnp.int32),
            pltpu.SMEM((n, slot_lanes), jnp.int32),
            pltpu.VMEM((chunks, 128), jnp.int32),
            pltpu.SMEM((chunks, 128), jnp.int32),
            pltpu.VMEM((dv, rows), f32),
            pltpu.VMEM((dv, rows), f32),
            pltpu.VMEM((dp, rows), f32),
            pltpu.VMEM((rows, dp), bf16),
            pltpu.VMEM((side, 16, 128), f32),
            pltpu.VMEM((side, 16, 128), f32),
            pltpu.VMEM((bits, 8, 128), f32),
            pltpu.VMEM((bits, 8, 128), f32),
            pltpu.VMEM((side, side, rows, part), bf16),
            pltpu.VMEM((side, half, part), f32),
            pltpu.VMEM((side, half, part), f32),
            pltpu.VMEM((side, side, half, part), bf16),
            pltpu.VMEM((side, side, half, part), bf16),
            pltpu.VMEM((side, half, part), bf16),
            pltpu.VMEM((side, half, part), bf16),
            pltpu.VMEM((side, half, part), bf16),
            pltpu.VMEM((side, half, part), bf16),
            dma((8,)),
            pltpu.SemaphoreType.REGULAR,
            dma((side,)),
            dma((side,)),
            dma((side, side)),
            dma((side, side)),
            dma((n,)),
            dma((n,)),
            dma((n,)),
            dma((n,)),
            dma((side,)),
            dma((side,)),
            dma((side,)),
            dma((side,)),
            dma((bits,)),
            dma((bits,)),
            dma((side, side)),
            dma((side, side)),
            dma((side, side)),
            dma((side, side)),
            dma((side,)),
            dma((side,)),
            dma((side,)),
            dma((side,)),
        ],
        compiler_params=pltpu.CompilerParams(
            collective_id=0, has_side_effects=True, vmem_limit_bytes=60 * 1024 * 1024
        ),
    )(
        draft_ids.reshape(id_rows, 128),
        token_ids.reshape(1, rows),
        gain.reshape(part // 128, 128),
        hidden,
        target_logits.T,
        head_weight.T,
    )
    return d_hidden, loss.reshape(rows)


def solution(mesh):
    in_specs = (P("tok", "voc"), P("tok", "voc"), P("voc"), P(None, "voc"), P(), P("tok"))
    out_specs = (P("tok", "voc"), P("tok"))
    return jax.shard_map(
        per_device, mesh=mesh, in_specs=in_specs, out_specs=out_specs, check_vma=False
    )
```

```python
import functools
import math
import jax
import jax.numpy as jnp
from jax import lax
from jax.experimental import pallas as pl
from jax.experimental.pallas import tpu as pltpu
from jax.sharding import PartitionSpec as P

epsilon = 1e-05
MESH = pl.DeviceIdType.MESH
f32 = jnp.float32
bf16 = jnp.bfloat16
NT = (((1,), (1,)), ((), ()))


def up(value, unit):
    return -(-value // unit) * unit


def body(
    dims,
    ids_hbm,
    tok_hbm,
    gain_hbm,
    hid_hbm,
    x_hbm,
    w_hbm,
    dh_ref,
    loss_ref,
    ids_v,
    tok_v,
    gain_v,
    x_v,
    w_v,
    hall,
    nrm,
    table,
    stage,
    psend,
    precv,
    pwide,
    idm_v,
    key_v,
    col_v,
    slot_f,
    slot_v,
    slot_s,
    idx_v,
    idx_s,
    lt,
    pt,
    wide_grad,
    grad,
    stat_x,
    stat_y,
    cross_x,
    cross_y,
    count,
    count_all,
    gsend,
    own_a,
    own_b,
    g1a,
    g1b,
    send_a,
    send_b,
    g2a,
    g2b,
    local_sem,
    entered,
    greeted,
    ha_first,
    hb_first,
    ha_next,
    hb_next,
    ha_recv,
    hb_recv,
    p_send,
    p_recv,
    sx_send,
    sx_recv,
    sy_send,
    sy_recv,
    tx_send,
    tx_recv,
    ty_send,
    ty_recv,
    c_send,
    c_recv,
    t_send,
    t_recv,
    ga_send,
    gb_send,
    g1a_recv,
    g1b_recv,
    g2a_send,
    g2b_send,
    g2a_recv,
    g2b_recv,
):
    n, m, vd, dv, cap = dims
    side = math.isqrt(n)
    part = hall.shape[2]
    rows = nrm.shape[0]
    half = rows // 2
    width = n * part
    chunks = idx_v.shape[0]
    slots = psend.shape[1]
    i = lax.axis_index("tok")
    j = lax.axis_index("voc")
    x = j // side
    y = lax.rem(j, side)

    def along_x(step):
        return lax.rem(x + step, side)

    def along_y(step):
        return lax.rem(y + step, side)

    copy_ids = pltpu.make_async_copy(ids_hbm, ids_v, local_sem.at[0])
    copy_hid = pltpu.make_async_copy(hid_hbm, hall.at[j, 0:rows], local_sem.at[1])
    copy_gain = pltpu.make_async_copy(gain_hbm, gain_v, local_sem.at[2])
    copy_tok = pltpu.make_async_copy(tok_hbm, tok_v, local_sem.at[3])
    copy_x = pltpu.make_async_copy(x_hbm, x_v, local_sem.at[4])
    copy_w = pltpu.make_async_copy(w_hbm, w_v, local_sem.at[5])
    copy_ids.start()
    copy_hid.start()
    copy_gain.start()
    copy_tok.start()
    copy_x.start()
    copy_w.start()

    barrier = pltpu.get_barrier_semaphore()
    hub = j == 0

    def greet(step, _):
        for peer in (along_x(step) * side + y, x * side + along_y(step)):

            @pl.when(peer != 0)
            def _():
                pl.semaphore_signal(barrier, inc=1, device_id=(i, peer), device_id_type=MESH)

        return 0

    lax.fori_loop(1, side, greet, 0)

    @pl.when(hub)
    def _():
        def greet_tok(step, _):
            peer = lax.rem(i + step, m)
            pl.semaphore_signal(barrier, inc=1, device_id=(peer, j), device_id_type=MESH)
            return 0

        lax.fori_loop(1, m, greet_tok, 0)


    copy_ids.wait()
    lane = lax.broadcasted_iota(jnp.int32, (chunks, 128), 1)
    entry = lax.broadcasted_iota(jnp.int32, (chunks, 128), 0) * 128 + lane
    total_rows = ids_v.shape[0]
    for k in range(n):
        first, shift = divmod(k * dv, 128)
        piece = ids_v[first : min(first + chunks + 1, total_rows), :].astype(f32)
        if shift:
            piece = pltpu.roll(piece, 128 - shift, 1)
        if piece.shape[0] == chunks:
            piece = jnp.concatenate([piece, piece[0:1, :]], axis=0)
        early = jnp.where(lane < 128 - shift, piece[0:chunks, :], piece[1 : chunks + 1, :])
        idm_v[k * chunks : (k + 1) * chunks, :] = jnp.where(entry < dv, early, -1.0)
    ids = idm_v[...]
    low = (j * vd).astype(f32)
    mine = ((ids >= low) & (ids < low + vd)).astype(f32)
    own = idm_v[pl.ds(pl.multiple_of(j * chunks, chunks), chunks), :]
    home = jnp.zeros_like(own)
    for k in range(1, n):
        home += (own >= float(k * vd)).astype(f32)
    home_all = jnp.concatenate([home] * n, axis=0)
    tall = (n * chunks, 128)
    row_shard = (lax.broadcasted_iota(jnp.int32, tall, 0) // chunks).astype(f32)
    hit = (home_all == row_shard).astype(f32)
    before = (
        lax.broadcasted_iota(jnp.int32, (128, 128), 0)
        < lax.broadcasted_iota(jnp.int32, (128, 128), 1)
    ).astype(f32).astype(bf16)
    ones = jnp.ones((128, 128), bf16)
    square_rows = (n * chunks, n * chunks)
    at_row = lax.broadcasted_iota(jnp.int32, square_rows, 0)
    at_column = lax.broadcasted_iota(jnp.int32, square_rows, 1)
    earlier = (
        (at_column < at_row) & (at_column >= at_row - at_row % chunks)
    ).astype(f32).astype(bf16)

    def ranks(mask):
        mask = mask.astype(bf16)
        ahead = jnp.dot(earlier, mask, preferred_element_type=f32).astype(bf16)
        return jnp.dot(mask, before, preferred_element_type=f32) + jnp.dot(
            ahead, ones, preferred_element_type=f32
        )

    key_v[...] = jnp.where(mine > 0.5, ranks(mine), -1.0)
    col_v[...] = ids - low
    rank_hit = ranks(hit) * hit
    rank_own = rank_hit[0:chunks, :]
    for k in range(1, n):
        rank_own += rank_hit[k * chunks : (k + 1) * chunks, :]
    idx_v[...] = jnp.clip((home * slots + rank_own).astype(jnp.int32), 0, n * slots - 1)

    copy_hid.wait()
    copy_gain.wait()
    wide_gain = gain_v[...].astype(f32)
    wide_gain = jnp.concatenate([wide_gain[r : r + 1, :] for r in range(part // 128)], axis=1)
    hall[j, rows : rows + 16, :] = jnp.broadcast_to(wide_gain, (16, part)).astype(bf16)

    @pl.when(j != 0)
    def _():
        pl.semaphore_wait(barrier, 2 * (side - 1))

    @pl.when((j != 0) & ((x == 0) | (y == 0)))
    def _():
        pl.semaphore_signal(greeted, inc=1, device_id=(i, 0), device_id_type=MESH)

    @pl.when(hub)
    def _():
        pl.semaphore_wait(greeted, 2 * (side - 1))

    def ha_copy(block, to_x, to_y, send_sem):
        piece = hall.at[block, 0:half]
        return pltpu.make_async_remote_copy(
            src_ref=piece,
            dst_ref=piece,
            send_sem=send_sem,
            recv_sem=ha_recv.at[block],
            device_id=(i, to_x * side + to_y),
            device_id_type=MESH,
        )

    def hb_copy(block, to_x, to_y, send_sem):
        piece = hall.at[block, half : rows + 16]
        return pltpu.make_async_remote_copy(
            src_ref=piece,
            dst_ref=piece,
            send_sem=send_sem,
            recv_sem=hb_recv.at[block],
            device_id=(i, to_x * side + to_y),
            device_id_type=MESH,
        )

    def ha_forward(from_x, step):
        to_y = along_y(step)
        return ha_copy(from_x * side + y, x, to_y, ha_next.at[from_x, to_y])

    def hb_forward(from_y, step):
        to_x = along_x(step)
        return hb_copy(x * side + from_y, to_x, y, hb_next.at[from_y, to_x])

    def h_first(step, _):
        ha_copy(j, along_x(step), y, ha_first.at[along_x(step)]).start()
        hb_copy(j, x, along_y(step), hb_first.at[along_y(step)]).start()
        return 0

    def h_own(step, _):
        ha_forward(x, step).start()
        hb_forward(y, step).start()
        pl.semaphore_signal(
            entered, inc=1, device_id=(i, x * side + along_y(step)), device_id_type=MESH
        )
        return 0

    lax.fori_loop(1, side, h_first, 0)
    lax.fori_loop(1, side, h_own, 0)

    slot_row = lax.broadcasted_iota(jnp.int32, (slots, 128), 0).astype(f32)
    slot_lane = lax.broadcasted_iota(jnp.int32, (slots, 128), 1)

    def slot_step(k, acc):
        at = pl.multiple_of(k * chunks, chunks)
        keys = key_v[pl.ds(at, chunks), :]
        cols = col_v[pl.ds(at, chunks), :]
        found = jnp.zeros((slots, 128), f32)
        for c in range(chunks):
            found = jnp.where(slot_row == keys[c : c + 1, :], cols[c : c + 1, :] - vd, found)
        return jnp.where(slot_lane == k, jnp.sum(found, axis=1, keepdims=True), acc)

    slot_f[...] = jnp.zeros_like(slot_f)
    slot_f[0:slots, :] = lax.fori_loop(0, n, slot_step, jnp.zeros((slots, 128), f32))
    slot_v[...] = jnp.clip(slot_f[...].T[0:n, :].astype(jnp.int32) + vd, 0, vd)
    copy_slot = pltpu.make_async_copy(slot_v, slot_s, local_sem.at[6])
    copy_idx = pltpu.make_async_copy(idx_v, idx_s, local_sem.at[7])
    copy_slot.start()
    copy_idx.start()

    def h_pass(step, _):
        from_x = along_x(step)
        from_y = along_y(step)
        ha_forward(from_x, 1).wait_recv()
        for later in range(1, side):
            ha_forward(from_x, later).start()
        hb_forward(from_y, 1).wait_recv()
        for later in range(1, side):
            hb_forward(from_y, later).start()
        return 0

    lax.fori_loop(1, side, h_pass, 0)

    copy_tok.wait()
    token_rows = jnp.broadcast_to(tok_v[...].astype(f32), (rows, rows)).T

    def valid_step(k, acc):
        entries = idm_v[pl.ds(pl.multiple_of(k * chunks, chunks), chunks), :]
        for c in range(chunks):
            acc = jnp.where(entries[c : c + 1, :] == token_rows, 1.0, acc)
        return acc

    valid = lax.fori_loop(0, n, valid_step, jnp.zeros((rows, 128), f32))
    valid = jnp.max(valid.T, axis=0, keepdims=True)

    def c_copy(slot, peer):
        return pltpu.make_async_remote_copy(
            src_ref=count.at[i],
            dst_ref=count.at[slot],
            send_sem=c_send.at[peer],
            recv_sem=c_recv.at[slot],
            device_id=(peer, j),
            device_id_type=MESH,
        )

    def t_copy(peer):
        return pltpu.make_async_remote_copy(
            src_ref=count_all,
            dst_ref=count_all,
            send_sem=t_send.at[peer],
            recv_sem=t_recv,
            device_id=(i, peer),
            device_id_type=MESH,
        )

    @pl.when(hub)
    def _():
        pl.semaphore_wait(barrier, m - 1)
        count[i] = jnp.broadcast_to(jnp.sum(valid, axis=1, keepdims=True), (8, 128))

        def c_start(step, _):
            c_copy(i, lax.rem(i + step, m)).start()
            return 0

        lax.fori_loop(1, m, c_start, 0)

    copy_x.wait()
    parts = 3
    span = vd // parts

    def widen_target(c, top):
        at = pl.multiple_of(c * span, 16)
        wide = x_v[pl.ds(at, span), :].astype(f32)
        table[pl.ds(at, span), :] = wide
        return jnp.maximum(top, jnp.max(wide, axis=0, keepdims=True))

    top_target = lax.fori_loop(0, parts, widen_target, jnp.full((1, rows), -1e30, f32))

    copy_slot.wait()
    copy_idx.wait()
    stage[...] = jnp.zeros_like(stage)
    table[vd : vd + 8, :] = jnp.full((8, rows), -1e30, f32)

    def p_copy(slot, peer):
        return pltpu.make_async_remote_copy(
            src_ref=psend.at[peer],
            dst_ref=precv.at[slot],
            send_sem=p_send.at[peer],
            recv_sem=p_recv.at[slot],
            device_id=(i, peer),
            device_id_type=MESH,
        )

    def pick(k):
        for at in range(cap):
            stage[at : at + 1, :] = table[pl.ds(slot_s[k, at], 1), :]
        return stage[...].astype(bf16)

    def pick_mass():
        return jnp.sum(jnp.exp(stage[0:cap, :] - top_target), axis=0, keepdims=True)

    def pick_step(step, acc):
        peer = lax.rem(j + step, n)
        psend[peer] = pick(peer)
        return acc + pick_mass()

    mass_here = lax.fori_loop(1, n, pick_step, jnp.zeros((1, rows), f32))
    precv[j] = pick(j)
    mass_here += pick_mass()

    total_target = lax.fori_loop(
        0,
        parts,
        lambda c, total: total
        + jnp.sum(
            jnp.exp(table[pl.ds(pl.multiple_of(c * span, 8), span), :] - top_target),
            axis=0,
            keepdims=True,
        ),
        jnp.zeros((1, rows), f32),
    )

    def h_rest(step, _):
        from_y = along_y(step)

        def h_rest_a(xs, _):
            ha_copy(xs * side + from_y, x, from_y, ha_next.at[0, 0]).wait_recv()
            return 0

        lax.fori_loop(0, side, h_rest_a, 0)
        from_x = along_x(step)

        def h_rest_b(ys, _):
            hb_copy(from_x * side + ys, from_x, y, hb_next.at[0, 0]).wait_recv()
            return 0

        lax.fori_loop(0, side, h_rest_b, 0)
        return 0

    lax.fori_loop(1, side, h_rest, 0)

    def p_start(step, _):
        p_copy(j, lax.rem(j + step, n)).start()
        return 0

    pl.semaphore_wait(entered, side - 1)
    lax.fori_loop(1, n, p_start, 0)

    def square(k, acc):
        wide = hall[k, 0:rows, :].astype(f32)
        return acc + wide * wide

    squares = lax.fori_loop(0, n, square, jnp.zeros((rows, part), f32))
    inv = lax.rsqrt(jnp.sum(squares, axis=1, keepdims=True) / width + epsilon)

    def normalise(k, _):
        wide = hall[k, 0:rows, :].astype(f32)
        gains = hall[k, rows : rows + 16, :].astype(f32)[0:1, :]
        at = pl.multiple_of(k * part, part)
        nrm[:, pl.ds(at, part)] = (wide * inv * gains).astype(bf16)
        return 0

    lax.fori_loop(0, n, normalise, 0)
    inv_row = jnp.broadcast_to(inv, (rows, 128)).T[0:1, :]

    copy_w.wait()
    lt[...] = lax.dot_general(w_v[...], nrm[...], NT, preferred_element_type=f32)
    draft = lt[...]
    top_draft = jnp.max(draft, axis=0, keepdims=True)
    lifted = jnp.exp(draft - top_draft)
    total_draft = jnp.sum(lifted, axis=0, keepdims=True)
    cross_draft = jnp.sum(lifted * draft, axis=0, keepdims=True)

    tops = (top_target, top_target, top_draft, top_draft)
    sums = (total_target, mass_here, total_draft, cross_draft)
    stat_x[x] = jnp.zeros((16, 128), f32)
    for r in range(4):
        stat_x[x, r : r + 1, :] = tops[r]
        stat_x[x, 8 + r : 9 + r, :] = sums[r]

    @pl.when(hub)
    def _():
        def c_wait(step, _):
            c_copy(lax.rem(i + step, m), i).wait_recv()
            return 0

        lax.fori_loop(1, m, c_wait, 0)
        count_all[...] = jnp.sum(count[...], axis=0)

        def t_start(peer, _):
            t_copy(peer).start()
            return 0

        lax.fori_loop(1, n, t_start, 0)

    def sx_copy(slot, to_x):
        return pltpu.make_async_remote_copy(
            src_ref=stat_x.at[slot],
            dst_ref=stat_x.at[slot],
            send_sem=sx_send.at[to_x],
            recv_sem=sx_recv.at[slot],
            device_id=(i, to_x * side + y),
            device_id_type=MESH,
        )

    def sy_copy(slot, to_y):
        return pltpu.make_async_remote_copy(
            src_ref=stat_y.at[slot],
            dst_ref=stat_y.at[slot],
            send_sem=sy_send.at[to_y],
            recv_sem=sy_recv.at[slot],
            device_id=(i, x * side + to_y),
            device_id_type=MESH,
        )

    def merge(ref):
        top = ref[0, 0:8, :]
        for k in range(1, side):
            top = jnp.maximum(top, ref[k, 0:8, :])
        total = jnp.zeros((8, 128), f32)
        for k in range(side):
            total += ref[k, 8:16, :] * jnp.exp(ref[k, 0:8, :] - top)
        return top, total

    for step in range(1, side):
        sx_copy(x, along_x(step)).start()
    for step in range(1, side):
        sx_copy(along_x(step), x).wait_recv()
    top, total = merge(stat_x)
    stat_y[y, 0:8, :] = top
    stat_y[y, 8:16, :] = total
    for step in range(1, side):
        sy_copy(y, along_y(step)).start()
    for step in range(1, side):
        sy_copy(along_y(step), y).wait_recv()
    top, total = merge(stat_y)

    target_lse = top[0:1, :] + jnp.log(total[0:1, :])
    mass = total[1:2, :] * jnp.exp(top[1:2, :] - target_lse)
    draft_lse = top[2:3, :] + jnp.log(total[2:3, :])
    mean_draft = total[3:4, :] / total[2:3, :]
    wide_grad[dv:, :] = jnp.zeros((wide_grad.shape[0] - dv, rows), f32)
    wide_grad[0:dv, :] = mass * jnp.exp(lt[...] - draft_lse)

    def p_wait(step, _):
        p_copy(lax.rem(j + step, n), j).wait_recv()
        return 0

    lax.fori_loop(1, n, p_wait, 0)

    def widen(k, _):
        pwide[pl.ds(pl.multiple_of(k * slots, 8), slots), :] = precv[k].astype(f32)
        return 0

    lax.fori_loop(0, n, widen, 0)
    for at in range(dv):
        pt[at : at + 1, :] = pwide[pl.ds(idx_s[at // 128, at % 128], 1), :]
    @pl.when(j != 0)
    def _():
        t_copy(0).wait_recv()

    weight = valid * (float(rows * m) / count_all[0:1, :])
    probs = jnp.exp(pt[...] - target_lse)
    wide_grad[0:dv, :] = weight * (wide_grad[0:dv, :] - probs)
    grad[...] = wide_grad[...].T.astype(bf16)
    cross_x[x] = jnp.broadcast_to(jnp.sum(probs * lt[...], axis=0, keepdims=True), (8, rows))

    def tx_copy(slot, to_x):
        return pltpu.make_async_remote_copy(
            src_ref=cross_x.at[slot],
            dst_ref=cross_x.at[slot],
            send_sem=tx_send.at[to_x],
            recv_sem=tx_recv.at[slot],
            device_id=(i, to_x * side + y),
            device_id_type=MESH,
        )

    def ty_copy(slot, to_y):
        return pltpu.make_async_remote_copy(
            src_ref=cross_y.at[slot],
            dst_ref=cross_y.at[slot],
            send_sem=ty_send.at[to_y],
            recv_sem=ty_recv.at[slot],
            device_id=(i, x * side + to_y),
            device_id_type=MESH,
        )

    for step in range(1, side):
        tx_copy(x, along_x(step)).start()

    def term(to_x, to_y):
        at = pl.multiple_of((to_x * side + to_y) * part, part)
        return jnp.dot(grad[:, 0:dv], w_v[:, pl.ds(at, part)], preferred_element_type=f32)

    def g1a_copy(from_x, to_x, to_y):
        return pltpu.make_async_remote_copy(
            src_ref=gsend.at[to_x, to_y, 0:half],
            dst_ref=g1a.at[from_x, to_y],
            send_sem=ga_send.at[to_x, to_y],
            recv_sem=g1a_recv.at[from_x, to_y],
            device_id=(i, to_x * side + y),
            device_id_type=MESH,
        )

    def g1b_copy(from_y, to_x, to_y):
        return pltpu.make_async_remote_copy(
            src_ref=gsend.at[to_x, to_y, half:rows],
            dst_ref=g1b.at[from_y, to_x],
            send_sem=gb_send.at[to_x, to_y],
            recv_sem=g1b_recv.at[from_y, to_x],
            device_id=(i, x * side + to_y),
            device_id_type=MESH,
        )

    def g_both(t, _):
        to_x = along_x(t // (side - 1) + 1)
        to_y = along_y(t % (side - 1) + 1)
        gsend[to_x, to_y] = term(to_x, to_y).astype(bf16)
        g1a_copy(x, to_x, to_y).start()
        g1b_copy(y, to_x, to_y).start()
        return 0

    def g_column(step, _):
        to_x = along_x(step)
        value = term(to_x, y)
        gsend[to_x, y] = value.astype(bf16)
        g1a_copy(x, to_x, y).start()
        own_b[to_x] = value[half:rows, :]
        return 0

    def g_row(step, _):
        to_y = along_y(step)
        value = term(x, to_y)
        gsend[x, to_y] = value.astype(bf16)
        g1b_copy(y, x, to_y).start()
        own_a[to_y] = value[0:half, :]
        return 0

    lax.fori_loop(0, (side - 1) * (side - 1), g_both, 0)
    lax.fori_loop(1, side, g_column, 0)
    lax.fori_loop(1, side, g_row, 0)
    value = term(x, y)
    own_a[y] = value[0:half, :]
    own_b[x] = value[half:rows, :]

    for step in range(1, side):
        tx_copy(along_x(step), x).wait_recv()
    cross_y[y] = jnp.sum(cross_x[...], axis=0)
    for step in range(1, side):
        ty_copy(y, along_y(step)).start()

    def sum_a(to_y):
        acc = own_a[to_y]
        for step in range(1, side):
            from_x = along_x(step)
            g1a_copy(from_x, x, to_y).wait_recv()
            acc += g1a[from_x, to_y].astype(f32)
        return acc

    def sum_b(to_x):
        acc = own_b[to_x]
        for step in range(1, side):
            from_y = along_y(step)
            g1b_copy(from_y, to_x, y).wait_recv()
            acc += g1b[from_y, to_x].astype(f32)
        return acc

    def g2a_copy(from_y, to_y):
        return pltpu.make_async_remote_copy(
            src_ref=send_a.at[to_y],
            dst_ref=g2a.at[from_y],
            send_sem=g2a_send.at[to_y],
            recv_sem=g2a_recv.at[from_y],
            device_id=(i, x * side + to_y),
            device_id_type=MESH,
        )

    def g2b_copy(from_x, to_x):
        return pltpu.make_async_remote_copy(
            src_ref=send_b.at[to_x],
            dst_ref=g2b.at[from_x],
            send_sem=g2b_send.at[to_x],
            recv_sem=g2b_recv.at[from_x],
            device_id=(i, to_x * side + y),
            device_id_type=MESH,
        )

    def g_second(step, _):
        to_y = along_y(step)
        send_a[to_y] = sum_a(to_y).astype(bf16)
        g2a_copy(y, to_y).start()
        to_x = along_x(step)
        send_b[to_x] = sum_b(to_x).astype(bf16)
        g2b_copy(x, to_x).start()
        return 0

    lax.fori_loop(1, side, g_second, 0)
    for step in range(1, side):
        ty_copy(along_y(step), y).wait_recv()
    cross = jnp.sum(cross_y[...], axis=0)[0:1, :]
    loss_ref[...] = weight * (mass * draft_lse - cross)
    spread = weight * (mass * mean_draft - cross)
    shrink = inv_row * inv_row * spread / width
    shrink = jnp.broadcast_to(shrink, (rows, rows)).T[:, 0:1]
    first = sum_a(y)
    second = sum_b(x)
    for step in range(1, side):
        from_y = along_y(step)
        g2a_copy(from_y, y).wait_recv()
        first += g2a[from_y].astype(f32)
        from_x = along_x(step)
        g2b_copy(from_x, x).wait_recv()
        second += g2b[from_x].astype(f32)
    wide_hidden = hall[j, 0:rows, :].astype(f32)
    dh_ref[0:half, :] = (
        wide_gain * inv[0:half, :] * first - wide_hidden[0:half, :] * shrink[0:half, :]
    )
    dh_ref[half:rows, :] = (
        wide_gain * inv[half:rows, :] * second - wide_hidden[half:rows, :] * shrink[half:rows, :]
    )

    def finish_voc(step, _):
        peer = lax.rem(j + step, n)
        p_copy(j, peer).wait_send()
        return 0

    def finish_side(step, _):
        to_x = along_x(step)
        to_y = along_y(step)
        ha_copy(j, to_x, y, ha_first.at[to_x]).wait_send()
        hb_copy(j, x, to_y, hb_first.at[to_y]).wait_send()
        for origin in range(side):
            ha_forward(origin, step).wait_send()
            hb_forward(origin, step).wait_send()
        sx_copy(x, to_x).wait_send()
        sy_copy(y, to_y).wait_send()
        tx_copy(x, to_x).wait_send()
        ty_copy(y, to_y).wait_send()
        for other in range(side):
            g1a_copy(x, to_x, other).wait_send()
            g1b_copy(y, other, to_y).wait_send()
        g2a_copy(y, to_y).wait_send()
        g2b_copy(x, to_x).wait_send()
        return 0

    lax.fori_loop(1, n, finish_voc, 0)
    lax.fori_loop(1, side, finish_side, 0)

    @pl.when(hub)
    def _():
        def finish_tok(step, _):
            c_copy(i, lax.rem(i + step, m)).wait_send()
            return 0

        def finish_total(peer, _):
            t_copy(peer).wait_send()
            return 0

        lax.fori_loop(1, m, finish_tok, 0)
        lax.fori_loop(1, n, finish_total, 0)


def per_device(target_logits, hidden, gain, head_weight, draft_ids, token_ids):
    n = lax.axis_size("voc")
    m = lax.axis_size("tok")
    rows, part = hidden.shape
    vd = target_logits.shape[1]
    width, dv = head_weight.shape
    side = math.isqrt(n)
    half = rows // 2
    cap = 8 * (5 * dv // (16 * n))
    slots = up(cap, 16)
    dp = up(dv, 128)
    chunks = dp // 128
    slot_lanes = up(slots, 128)
    id_rows = n * dv // 128
    vmem = pl.BlockSpec(memory_space=pltpu.VMEM)
    anywhere = pl.BlockSpec(memory_space=pl.ANY)
    dma = pltpu.SemaphoreType.DMA
    d_hidden, loss = pl.pallas_call(
        functools.partial(body, (n, m, vd, dv, cap)),
        out_shape=(
            jax.ShapeDtypeStruct((rows, part), f32),
            jax.ShapeDtypeStruct((1, rows), f32),
        ),
        in_specs=[anywhere] * 6,
        out_specs=(vmem, vmem),
        scratch_shapes=[
            pltpu.VMEM((id_rows, 128), jnp.int32),
            pltpu.VMEM((1, rows), jnp.int32),
            pltpu.VMEM((part // 128, 128), bf16),
            pltpu.VMEM((vd, rows), bf16),
            pltpu.VMEM((dv, width), bf16),
            pltpu.VMEM((n, rows + 16, part), bf16),
            pltpu.VMEM((rows, width), bf16),
            pltpu.VMEM((vd + 8, rows), f32),
            pltpu.VMEM((slots, rows), f32),
            pltpu.VMEM((n, slots, rows), bf16),
            pltpu.VMEM((n, slots, rows), bf16),
            pltpu.VMEM((n * slots, rows), f32),
            pltpu.VMEM((n * chunks, 128), f32),
            pltpu.VMEM((n * chunks, 128), f32),
            pltpu.VMEM((n * chunks, 128), f32),
            pltpu.VMEM((slot_lanes, 128), f32),
            pltpu.VMEM((n, slot_lanes), jnp.int32),
            pltpu.SMEM((n, slot_lanes), jnp.int32),
            pltpu.VMEM((chunks, 128), jnp.int32),
            pltpu.SMEM((chunks, 128), jnp.int32),
            pltpu.VMEM((dv, rows), f32),
            pltpu.VMEM((dv, rows), f32),
            pltpu.VMEM((dp, rows), f32),
            pltpu.VMEM((rows, dp), bf16),
            pltpu.VMEM((side, 16, 128), f32),
            pltpu.VMEM((side, 16, 128), f32),
            pltpu.VMEM((side, 8, 128), f32),
            pltpu.VMEM((side, 8, 128), f32),
            pltpu.VMEM((m, 8, 128), f32),
            pltpu.VMEM((8, 128), f32),
            pltpu.VMEM((side, side, rows, part), bf16),
            pltpu.VMEM((side, half, part), f32),
            pltpu.VMEM((side, half, part), f32),
            pltpu.VMEM((side, side, half, part), bf16),
            pltpu.VMEM((side, side, half, part), bf16),
            pltpu.VMEM((side, half, part), bf16),
            pltpu.VMEM((side, half, part), bf16),
            pltpu.VMEM((side, half, part), bf16),
            pltpu.VMEM((side, half, part), bf16),
            dma((8,)),
            pltpu.SemaphoreType.REGULAR,
            pltpu.SemaphoreType.REGULAR,
            dma((side,)),
            dma((side,)),
            dma((side, side)),
            dma((side, side)),
            dma((n,)),
            dma((n,)),
            dma((n,)),
            dma((n,)),
            dma((side,)),
            dma((side,)),
            dma((side,)),
            dma((side,)),
            dma((side,)),
            dma((side,)),
            dma((side,)),
            dma((side,)),
            dma((m,)),
            dma((m,)),
            dma((n,)),
            dma,
            dma((side, side)),
            dma((side, side)),
            dma((side, side)),
            dma((side, side)),
            dma((side,)),
            dma((side,)),
            dma((side,)),
            dma((side,)),
        ],
        compiler_params=pltpu.CompilerParams(
            collective_id=0, has_side_effects=True, vmem_limit_bytes=60 * 1024 * 1024
        ),
    )(
        draft_ids.reshape(id_rows, 128),
        token_ids.reshape(1, rows),
        gain.reshape(part // 128, 128),
        hidden,
        target_logits.T,
        head_weight.T,
    )
    return d_hidden, loss.reshape(rows)


def solution(mesh):
    in_specs = (P("tok", "voc"), P("tok", "voc"), P("voc"), P(None, "voc"), P(), P("tok"))
    out_specs = (P("tok", "voc"), P("tok"))
    return jax.shard_map(
        per_device, mesh=mesh, in_specs=in_specs, out_specs=out_specs, check_vma=False
    )
```

```python
import functools
import math
import jax
import jax.numpy as jnp
from jax import lax
from jax.experimental import pallas as pl
from jax.experimental.pallas import tpu as pltpu
from jax.sharding import PartitionSpec as P

epsilon = 1e-05
MESH = pl.DeviceIdType.MESH
f32 = jnp.float32
bf16 = jnp.bfloat16
NT = (((1,), (1,)), ((), ()))


def up(value, unit):
    return -(-value // unit) * unit


def body(
    dims,
    ids_hbm,
    tok_hbm,
    gain_hbm,
    hid_hbm,
    x_hbm,
    w_hbm,
    dh_ref,
    loss_ref,
    ids_v,
    tok_v,
    gain_v,
    x_v,
    w_v,
    hall,
    nrm,
    table,
    stage,
    psend,
    precv,
    pwide,
    idm_v,
    key_v,
    col_v,
    slot_f,
    slot_v,
    slot_s,
    idx_v,
    idx_s,
    lt,
    pt,
    wide_grad,
    grad,
    stats,
    cross_x,
    cross_y,
    square_x,
    square_y,
    count,
    count_all,
    gsend,
    own_a,
    own_b,
    g1a,
    g1b,
    send_a,
    send_b,
    g2a,
    g2b,
    local_sem,
    entered,
    greeted,
    ha_first,
    hb_first,
    ha_next,
    hb_next,
    ha_recv,
    hb_recv,
    p_send,
    p_recv,
    s_send,
    s_recv,
    qx_send,
    qx_recv,
    qy_send,
    qy_recv,
    tx_send,
    tx_recv,
    ty_send,
    ty_recv,
    c_send,
    c_recv,
    t_send,
    t_recv,
    ga_send,
    gb_send,
    g1a_recv,
    g1b_recv,
    g2a_send,
    g2b_send,
    g2a_recv,
    g2b_recv,
):
    n, m, vd, dv, cap = dims
    side = math.isqrt(n)
    part = hall.shape[2]
    rows = nrm.shape[0]
    half = rows // 2
    width = n * part
    chunks = idx_v.shape[0]
    slots = psend.shape[1]
    i = lax.axis_index("tok")
    j = lax.axis_index("voc")
    x = j // side
    y = lax.rem(j, side)

    def along_x(step):
        return lax.rem(x + step, side)

    def along_y(step):
        return lax.rem(y + step, side)

    copy_ids = pltpu.make_async_copy(ids_hbm, ids_v, local_sem.at[0])
    copy_hid = pltpu.make_async_copy(hid_hbm, hall.at[j, 0:rows], local_sem.at[1])
    copy_gain = pltpu.make_async_copy(gain_hbm, gain_v, local_sem.at[2])
    copy_tok = pltpu.make_async_copy(tok_hbm, tok_v, local_sem.at[3])
    copy_x = pltpu.make_async_copy(x_hbm, x_v, local_sem.at[4])
    copy_w = pltpu.make_async_copy(w_hbm, w_v, local_sem.at[5])
    copy_ids.start()
    copy_hid.start()
    copy_gain.start()
    copy_tok.start()
    copy_x.start()
    copy_w.start()

    barrier = pltpu.get_barrier_semaphore()
    hub = j == 0

    def greet(step, _):
        for peer in (along_x(step) * side + y, x * side + along_y(step)):

            @pl.when(peer != 0)
            def _():
                pl.semaphore_signal(barrier, inc=1, device_id=(i, peer), device_id_type=MESH)

        return 0

    lax.fori_loop(1, side, greet, 0)

    @pl.when(hub)
    def _():
        def greet_tok(step, _):
            peer = lax.rem(i + step, m)
            pl.semaphore_signal(barrier, inc=1, device_id=(peer, j), device_id_type=MESH)
            return 0

        lax.fori_loop(1, m, greet_tok, 0)


    copy_ids.wait()
    lane = lax.broadcasted_iota(jnp.int32, (chunks, 128), 1)
    entry = lax.broadcasted_iota(jnp.int32, (chunks, 128), 0) * 128 + lane
    total_rows = ids_v.shape[0]
    for k in range(n):
        first, shift = divmod(k * dv, 128)
        piece = ids_v[first : min(first + chunks + 1, total_rows), :].astype(f32)
        if shift:
            piece = pltpu.roll(piece, 128 - shift, 1)
        if piece.shape[0] == chunks:
            piece = jnp.concatenate([piece, piece[0:1, :]], axis=0)
        early = jnp.where(lane < 128 - shift, piece[0:chunks, :], piece[1 : chunks + 1, :])
        idm_v[k * chunks : (k + 1) * chunks, :] = jnp.where(entry < dv, early, -1.0)
    ids = idm_v[...]
    low = (j * vd).astype(f32)
    mine = ((ids >= low) & (ids < low + vd)).astype(f32)
    own = idm_v[pl.ds(pl.multiple_of(j * chunks, chunks), chunks), :]
    home = jnp.zeros_like(own)
    for k in range(1, n):
        home += (own >= float(k * vd)).astype(f32)
    home_all = jnp.concatenate([home] * n, axis=0)
    tall = (n * chunks, 128)
    row_shard = (lax.broadcasted_iota(jnp.int32, tall, 0) // chunks).astype(f32)
    hit = (home_all == row_shard).astype(f32)
    before = (
        lax.broadcasted_iota(jnp.int32, (128, 128), 0)
        < lax.broadcasted_iota(jnp.int32, (128, 128), 1)
    ).astype(f32).astype(bf16)
    ones = jnp.ones((128, 128), bf16)
    square_rows = (n * chunks, n * chunks)
    at_row = lax.broadcasted_iota(jnp.int32, square_rows, 0)
    at_column = lax.broadcasted_iota(jnp.int32, square_rows, 1)
    earlier = (
        (at_column < at_row) & (at_column >= at_row - at_row % chunks)
    ).astype(f32).astype(bf16)

    def ranks(mask):
        mask = mask.astype(bf16)
        ahead = jnp.dot(earlier, mask, preferred_element_type=f32).astype(bf16)
        return jnp.dot(mask, before, preferred_element_type=f32) + jnp.dot(
            ahead, ones, preferred_element_type=f32
        )

    key_v[...] = jnp.where(mine > 0.5, ranks(mine), -1.0)
    col_v[...] = ids - low
    rank_hit = ranks(hit) * hit
    rank_own = rank_hit[0:chunks, :]
    for k in range(1, n):
        rank_own += rank_hit[k * chunks : (k + 1) * chunks, :]
    idx_v[...] = jnp.clip((home * slots + rank_own).astype(jnp.int32), 0, n * slots - 1)

    copy_hid.wait()
    copy_gain.wait()
    wide_gain = gain_v[...].astype(f32)
    wide_gain = jnp.concatenate([wide_gain[r : r + 1, :] for r in range(part // 128)], axis=1)

    @pl.when(j != 0)
    def _():
        pl.semaphore_wait(barrier, 2 * (side - 1))

    @pl.when((j != 0) & ((x == 0) | (y == 0)))
    def _():
        pl.semaphore_signal(greeted, inc=1, device_id=(i, 0), device_id_type=MESH)

    @pl.when(hub)
    def _():
        pl.semaphore_wait(greeted, 2 * (side - 1))

    def ha_copy(block, to_x, to_y, send_sem):
        piece = hall.at[block, 0:half]
        return pltpu.make_async_remote_copy(
            src_ref=piece,
            dst_ref=piece,
            send_sem=send_sem,
            recv_sem=ha_recv.at[block],
            device_id=(i, to_x * side + to_y),
            device_id_type=MESH,
        )

    def hb_copy(block, to_x, to_y, send_sem):
        piece = hall.at[block, half:rows]
        return pltpu.make_async_remote_copy(
            src_ref=piece,
            dst_ref=piece,
            send_sem=send_sem,
            recv_sem=hb_recv.at[block],
            device_id=(i, to_x * side + to_y),
            device_id_type=MESH,
        )

    def ha_forward(from_x, step):
        to_y = along_y(step)
        return ha_copy(from_x * side + y, x, to_y, ha_next.at[from_x, to_y])

    def hb_forward(from_y, step):
        to_x = along_x(step)
        return hb_copy(x * side + from_y, to_x, y, hb_next.at[from_y, to_x])

    def h_first(step, _):
        ha_copy(j, along_x(step), y, ha_first.at[along_x(step)]).start()
        hb_copy(j, x, along_y(step), hb_first.at[along_y(step)]).start()
        return 0

    def h_own(step, _):
        ha_forward(x, step).start()
        hb_forward(y, step).start()
        pl.semaphore_signal(
            entered, inc=1, device_id=(i, x * side + along_y(step)), device_id_type=MESH
        )
        return 0

    lax.fori_loop(1, side, h_first, 0)
    lax.fori_loop(1, side, h_own, 0)

    own_hidden = hall[j, 0:rows, :].astype(f32)
    own_squares = jnp.sum(own_hidden * own_hidden, axis=1, keepdims=True)
    square_x[x] = jnp.broadcast_to(own_squares, (rows, 128)).T[0:8, :]
    square_x[x, 1 : 1 + part // 128, :] = gain_v[...].astype(f32)

    def qx_copy(slot, to_x):
        return pltpu.make_async_remote_copy(
            src_ref=square_x.at[slot],
            dst_ref=square_x.at[slot],
            send_sem=qx_send.at[to_x],
            recv_sem=qx_recv.at[slot],
            device_id=(i, to_x * side + y),
            device_id_type=MESH,
        )

    def qy_copy(slot, to_y):
        return pltpu.make_async_remote_copy(
            src_ref=square_y.at[slot],
            dst_ref=square_y.at[slot],
            send_sem=qy_send.at[to_y],
            recv_sem=qy_recv.at[slot],
            device_id=(i, x * side + to_y),
            device_id_type=MESH,
        )

    for step in range(1, side):
        qx_copy(x, along_x(step)).start()

    slot_row = lax.broadcasted_iota(jnp.int32, (slots, 128), 0).astype(f32)
    slot_lane = lax.broadcasted_iota(jnp.int32, (slots, 128), 1)

    def slot_step(k, acc):
        at = pl.multiple_of(k * chunks, chunks)
        keys = key_v[pl.ds(at, chunks), :]
        cols = col_v[pl.ds(at, chunks), :]
        found = jnp.zeros((slots, 128), f32)
        for c in range(chunks):
            found = jnp.where(slot_row == keys[c : c + 1, :], cols[c : c + 1, :] - vd, found)
        return jnp.where(slot_lane == k, jnp.sum(found, axis=1, keepdims=True), acc)

    slot_f[...] = jnp.zeros_like(slot_f)
    slot_f[0:slots, :] = lax.fori_loop(0, n, slot_step, jnp.zeros((slots, 128), f32))
    slot_v[...] = jnp.clip(slot_f[...].T[0:n, :].astype(jnp.int32) + vd, 0, vd)
    copy_slot = pltpu.make_async_copy(slot_v, slot_s, local_sem.at[6])
    copy_idx = pltpu.make_async_copy(idx_v, idx_s, local_sem.at[7])
    copy_slot.start()
    copy_idx.start()

    def h_pass(step, _):
        from_x = along_x(step)
        from_y = along_y(step)
        ha_forward(from_x, 1).wait_recv()
        for later in range(1, side):
            ha_forward(from_x, later).start()
        hb_forward(from_y, 1).wait_recv()
        for later in range(1, side):
            hb_forward(from_y, later).start()
        return 0

    lax.fori_loop(1, side, h_pass, 0)
    for step in range(1, side):
        qx_copy(along_x(step), x).wait_recv()
    square_y[y] = square_x[...]
    for step in range(1, side):
        qy_copy(y, along_y(step)).start()

    copy_tok.wait()
    token_rows = jnp.broadcast_to(tok_v[...].astype(f32), (rows, rows)).T

    def valid_step(k, acc):
        entries = idm_v[pl.ds(pl.multiple_of(k * chunks, chunks), chunks), :]
        for c in range(chunks):
            acc = jnp.where(entries[c : c + 1, :] == token_rows, 1.0, acc)
        return acc

    valid = lax.fori_loop(0, n, valid_step, jnp.zeros((rows, 128), f32))
    valid = jnp.max(valid.T, axis=0, keepdims=True)

    def c_copy(slot, peer):
        return pltpu.make_async_remote_copy(
            src_ref=count.at[i],
            dst_ref=count.at[slot],
            send_sem=c_send.at[peer],
            recv_sem=c_recv.at[slot],
            device_id=(peer, j),
            device_id_type=MESH,
        )

    def t_copy(peer):
        return pltpu.make_async_remote_copy(
            src_ref=count_all,
            dst_ref=count_all,
            send_sem=t_send.at[peer],
            recv_sem=t_recv,
            device_id=(i, peer),
            device_id_type=MESH,
        )

    @pl.when(hub)
    def _():
        pl.semaphore_wait(barrier, m - 1)
        count[i] = jnp.broadcast_to(jnp.sum(valid, axis=1, keepdims=True), (8, 128))

        def c_start(step, _):
            c_copy(i, lax.rem(i + step, m)).start()
            return 0

        lax.fori_loop(1, m, c_start, 0)

    copy_x.wait()
    parts = 3
    span = vd // parts

    def widen_target(c, top):
        at = pl.multiple_of(c * span, 16)
        wide = x_v[pl.ds(at, span), :].astype(f32)
        table[pl.ds(at, span), :] = wide
        return jnp.maximum(top, jnp.max(wide, axis=0, keepdims=True))

    top_target = lax.fori_loop(0, parts, widen_target, jnp.full((1, rows), -1e30, f32))

    copy_slot.wait()
    copy_idx.wait()
    stage[...] = jnp.zeros_like(stage)
    table[vd : vd + 8, :] = jnp.full((8, rows), -1e30, f32)

    def p_copy(slot, peer):
        return pltpu.make_async_remote_copy(
            src_ref=psend.at[peer],
            dst_ref=precv.at[slot],
            send_sem=p_send.at[peer],
            recv_sem=p_recv.at[slot],
            device_id=(i, peer),
            device_id_type=MESH,
        )

    def pick(k):
        for at in range(cap):
            stage[at : at + 1, :] = table[pl.ds(slot_s[k, at], 1), :]
        return stage[...].astype(bf16)

    def pick_mass():
        return jnp.sum(jnp.exp(stage[0:cap, :] - top_target), axis=0, keepdims=True)

    def pick_step(step, acc):
        peer = lax.rem(j + step, n)
        psend[peer] = pick(peer)
        return acc + pick_mass()

    mass_here = lax.fori_loop(1, n, pick_step, jnp.zeros((1, rows), f32))
    precv[j] = pick(j)
    mass_here += pick_mass()

    total_target = lax.fori_loop(
        0,
        parts,
        lambda c, total: total
        + jnp.sum(
            jnp.exp(table[pl.ds(pl.multiple_of(c * span, 8), span), :] - top_target),
            axis=0,
            keepdims=True,
        ),
        jnp.zeros((1, rows), f32),
    )

    for step in range(1, side):
        qy_copy(along_y(step), y).wait_recv()
    squares = jnp.sum(jnp.sum(square_y[...], axis=0), axis=0)[0:1, :]
    inv_row = lax.rsqrt(squares / width + epsilon)
    inv = jnp.broadcast_to(inv_row, (rows, rows)).T[:, 0:1]

    def p_start(step, _):
        p_copy(j, lax.rem(j + step, n)).start()
        return 0

    def normalise(xs, ys):
        k = xs * side + ys
        wide = hall[k, 0:rows, :].astype(f32)
        tile = square_y[ys, xs]
        gains = jnp.concatenate([tile[r + 1 : r + 2, :] for r in range(part // 128)], axis=1)
        at = pl.multiple_of(k * part, part)
        nrm[:, pl.ds(at, part)] = (wide * inv * gains).astype(bf16)

    for step in range(side):
        from_x = along_x(step)
        for other in range(1, side):
            from_y = along_y(other)
            ha_copy(from_x * side + from_y, x, from_y, ha_next.at[0, 0]).wait_recv()
        if step:
            for other in range(side):
                hb_copy(from_x * side + other, from_x, y, hb_next.at[0, 0]).wait_recv()
        if step == 0:
            pl.semaphore_wait(entered, side - 1)
            lax.fori_loop(1, n, p_start, 0)
        for other in range(side):
            normalise(from_x, other)
        if step == 0:
            copy_w.wait()
        at = pl.ds(pl.multiple_of(from_x * side * part, part), side * part)
        share = lax.dot_general(w_v[:, at], nrm[:, at], NT, preferred_element_type=f32)
        if step:
            lt[...] += share
        else:
            lt[...] = share

    draft = lt[...]
    top_draft = jnp.max(draft, axis=0, keepdims=True)
    lifted = jnp.exp(draft - top_draft)
    total_draft = jnp.sum(lifted, axis=0, keepdims=True)
    cross_draft = jnp.sum(lifted * draft, axis=0, keepdims=True)

    tops = (top_target, top_target, top_draft, top_draft)
    sums = (total_target, mass_here, total_draft, cross_draft)
    stats[j] = jnp.zeros((16, 128), f32)
    for r in range(4):
        stats[j, r : r + 1, :] = tops[r]
        stats[j, 8 + r : 9 + r, :] = sums[r]

    @pl.when(hub)
    def _():
        def c_wait(step, _):
            c_copy(lax.rem(i + step, m), i).wait_recv()
            return 0

        lax.fori_loop(1, m, c_wait, 0)
        count_all[...] = jnp.sum(count[...], axis=0)

        def t_start(peer, _):
            t_copy(peer).start()
            return 0

        lax.fori_loop(1, n, t_start, 0)

    def s_copy(slot, peer):
        return pltpu.make_async_remote_copy(
            src_ref=stats.at[slot],
            dst_ref=stats.at[slot],
            send_sem=s_send.at[peer],
            recv_sem=s_recv.at[slot],
            device_id=(i, peer),
            device_id_type=MESH,
        )

    def merge(ref):
        top = ref[0, 0:8, :]
        for k in range(1, n):
            top = jnp.maximum(top, ref[k, 0:8, :])
        total = jnp.zeros((8, 128), f32)
        for k in range(n):
            total += ref[k, 8:16, :] * jnp.exp(ref[k, 0:8, :] - top)
        return top, total

    def s_start(step, _):
        s_copy(j, lax.rem(j + step, n)).start()
        return 0

    def s_wait(step, _):
        s_copy(lax.rem(j + step, n), j).wait_recv()
        return 0

    lax.fori_loop(1, n, s_start, 0)
    lax.fori_loop(1, n, s_wait, 0)
    top, total = merge(stats)

    target_lse = top[0:1, :] + jnp.log(total[0:1, :])
    mass = total[1:2, :] * jnp.exp(top[1:2, :] - target_lse)
    draft_lse = top[2:3, :] + jnp.log(total[2:3, :])
    mean_draft = total[3:4, :] / total[2:3, :]
    wide_grad[dv:, :] = jnp.zeros((wide_grad.shape[0] - dv, rows), f32)
    wide_grad[0:dv, :] = mass * jnp.exp(lt[...] - draft_lse)

    def widen(k):
        pwide[pl.ds(pl.multiple_of(k * slots, 8), slots), :] = precv[k].astype(f32)

    def p_wait(step, _):
        slot = lax.rem(j + step, n)
        p_copy(slot, j).wait_recv()
        widen(slot)
        return 0

    widen(j)
    lax.fori_loop(1, n, p_wait, 0)
    for at in range(dv):
        pt[at : at + 1, :] = pwide[pl.ds(idx_s[at // 128, at % 128], 1), :]
    @pl.when(j != 0)
    def _():
        t_copy(0).wait_recv()

    weight = valid * (float(rows * m) / count_all[0:1, :])
    probs = jnp.exp(pt[...] - target_lse)
    wide_grad[0:dv, :] = weight * (wide_grad[0:dv, :] - probs)
    grad[...] = wide_grad[...].T.astype(bf16)
    cross_x[x] = jnp.broadcast_to(jnp.sum(probs * lt[...], axis=0, keepdims=True), (8, rows))

    def tx_copy(slot, to_x):
        return pltpu.make_async_remote_copy(
            src_ref=cross_x.at[slot],
            dst_ref=cross_x.at[slot],
            send_sem=tx_send.at[to_x],
            recv_sem=tx_recv.at[slot],
            device_id=(i, to_x * side + y),
            device_id_type=MESH,
        )

    def ty_copy(slot, to_y):
        return pltpu.make_async_remote_copy(
            src_ref=cross_y.at[slot],
            dst_ref=cross_y.at[slot],
            send_sem=ty_send.at[to_y],
            recv_sem=ty_recv.at[slot],
            device_id=(i, x * side + to_y),
            device_id_type=MESH,
        )

    for step in range(1, side):
        tx_copy(x, along_x(step)).start()

    def term(to_x, to_y):
        at = pl.multiple_of((to_x * side + to_y) * part, part)
        return jnp.dot(grad[:, 0:dv], w_v[:, pl.ds(at, part)], preferred_element_type=f32)

    def g1a_copy(from_x, to_x, to_y):
        return pltpu.make_async_remote_copy(
            src_ref=gsend.at[to_x, to_y, 0:half],
            dst_ref=g1a.at[from_x, to_y],
            send_sem=ga_send.at[to_x, to_y],
            recv_sem=g1a_recv.at[from_x, to_y],
            device_id=(i, to_x * side + y),
            device_id_type=MESH,
        )

    def g1b_copy(from_y, to_x, to_y):
        return pltpu.make_async_remote_copy(
            src_ref=gsend.at[to_x, to_y, half:rows],
            dst_ref=g1b.at[from_y, to_x],
            send_sem=gb_send.at[to_x, to_y],
            recv_sem=g1b_recv.at[from_y, to_x],
            device_id=(i, x * side + to_y),
            device_id_type=MESH,
        )

    def g_both(t, _):
        to_x = along_x(t // (side - 1) + 1)
        to_y = along_y(t % (side - 1) + 1)
        gsend[to_x, to_y] = term(to_x, to_y).astype(bf16)
        g1a_copy(x, to_x, to_y).start()
        g1b_copy(y, to_x, to_y).start()
        return 0

    def g_column(step, _):
        to_x = along_x(step)
        value = term(to_x, y)
        gsend[to_x, y] = value.astype(bf16)
        g1a_copy(x, to_x, y).start()
        own_b[to_x] = value[half:rows, :]
        return 0

    def g_row(step, _):
        to_y = along_y(step)
        value = term(x, to_y)
        gsend[x, to_y] = value.astype(bf16)
        g1b_copy(y, x, to_y).start()
        own_a[to_y] = value[0:half, :]
        return 0

    lax.fori_loop(0, (side - 1) * (side - 1), g_both, 0)
    lax.fori_loop(1, side, g_column, 0)
    lax.fori_loop(1, side, g_row, 0)
    value = term(x, y)
    own_a[y] = value[0:half, :]
    own_b[x] = value[half:rows, :]

    for step in range(1, side):
        tx_copy(along_x(step), x).wait_recv()
    cross_y[y] = jnp.sum(cross_x[...], axis=0)
    for step in range(1, side):
        ty_copy(y, along_y(step)).start()

    def sum_a(to_y):
        acc = own_a[to_y]
        for step in range(1, side):
            from_x = along_x(step)
            g1a_copy(from_x, x, to_y).wait_recv()
            acc += g1a[from_x, to_y].astype(f32)
        return acc

    def sum_b(to_x):
        acc = own_b[to_x]
        for step in range(1, side):
            from_y = along_y(step)
            g1b_copy(from_y, to_x, y).wait_recv()
            acc += g1b[from_y, to_x].astype(f32)
        return acc

    def g2a_copy(from_y, to_y):
        return pltpu.make_async_remote_copy(
            src_ref=send_a.at[to_y],
            dst_ref=g2a.at[from_y],
            send_sem=g2a_send.at[to_y],
            recv_sem=g2a_recv.at[from_y],
            device_id=(i, x * side + to_y),
            device_id_type=MESH,
        )

    def g2b_copy(from_x, to_x):
        return pltpu.make_async_remote_copy(
            src_ref=send_b.at[to_x],
            dst_ref=g2b.at[from_x],
            send_sem=g2b_send.at[to_x],
            recv_sem=g2b_recv.at[from_x],
            device_id=(i, to_x * side + y),
            device_id_type=MESH,
        )

    def g_second(step, _):
        to_y = along_y(step)
        send_a[to_y] = sum_a(to_y).astype(bf16)
        g2a_copy(y, to_y).start()
        to_x = along_x(step)
        send_b[to_x] = sum_b(to_x).astype(bf16)
        g2b_copy(x, to_x).start()
        return 0

    lax.fori_loop(1, side, g_second, 0)
    for step in range(1, side):
        ty_copy(along_y(step), y).wait_recv()
    cross = jnp.sum(cross_y[...], axis=0)[0:1, :]
    loss_ref[...] = weight * (mass * draft_lse - cross)
    spread = weight * (mass * mean_draft - cross)
    shrink = inv_row * inv_row * spread / width
    shrink = jnp.broadcast_to(shrink, (rows, rows)).T[:, 0:1]
    first = sum_a(y)
    second = sum_b(x)
    for step in range(1, side):
        from_y = along_y(step)
        g2a_copy(from_y, y).wait_recv()
        first += g2a[from_y].astype(f32)
        from_x = along_x(step)
        g2b_copy(from_x, x).wait_recv()
        second += g2b[from_x].astype(f32)
    wide_hidden = hall[j, 0:rows, :].astype(f32)
    dh_ref[0:half, :] = (
        wide_gain * inv[0:half, :] * first - wide_hidden[0:half, :] * shrink[0:half, :]
    )
    dh_ref[half:rows, :] = (
        wide_gain * inv[half:rows, :] * second - wide_hidden[half:rows, :] * shrink[half:rows, :]
    )

    def finish_voc(step, _):
        peer = lax.rem(j + step, n)
        p_copy(j, peer).wait_send()
        s_copy(j, peer).wait_send()
        return 0

    def finish_side(step, _):
        to_x = along_x(step)
        to_y = along_y(step)
        ha_copy(j, to_x, y, ha_first.at[to_x]).wait_send()
        hb_copy(j, x, to_y, hb_first.at[to_y]).wait_send()
        for origin in range(side):
            ha_forward(origin, step).wait_send()
            hb_forward(origin, step).wait_send()
        qx_copy(x, to_x).wait_send()
        qy_copy(y, to_y).wait_send()
        tx_copy(x, to_x).wait_send()
        ty_copy(y, to_y).wait_send()
        for other in range(side):
            g1a_copy(x, to_x, other).wait_send()
            g1b_copy(y, other, to_y).wait_send()
        g2a_copy(y, to_y).wait_send()
        g2b_copy(x, to_x).wait_send()
        return 0

    lax.fori_loop(1, n, finish_voc, 0)
    lax.fori_loop(1, side, finish_side, 0)

    @pl.when(hub)
    def _():
        def finish_tok(step, _):
            c_copy(i, lax.rem(i + step, m)).wait_send()
            return 0

        def finish_total(peer, _):
            t_copy(peer).wait_send()
            return 0

        lax.fori_loop(1, m, finish_tok, 0)
        lax.fori_loop(1, n, finish_total, 0)


def per_device(target_logits, hidden, gain, head_weight, draft_ids, token_ids):
    n = lax.axis_size("voc")
    m = lax.axis_size("tok")
    rows, part = hidden.shape
    vd = target_logits.shape[1]
    width, dv = head_weight.shape
    side = math.isqrt(n)
    half = rows // 2
    cap = 8 * (5 * dv // (16 * n))
    slots = up(cap, 16)
    dp = up(dv, 128)
    chunks = dp // 128
    slot_lanes = up(slots, 128)
    id_rows = n * dv // 128
    vmem = pl.BlockSpec(memory_space=pltpu.VMEM)
    anywhere = pl.BlockSpec(memory_space=pl.ANY)
    dma = pltpu.SemaphoreType.DMA
    d_hidden, loss = pl.pallas_call(
        functools.partial(body, (n, m, vd, dv, cap)),
        out_shape=(
            jax.ShapeDtypeStruct((rows, part), f32),
            jax.ShapeDtypeStruct((1, rows), f32),
        ),
        in_specs=[anywhere] * 6,
        out_specs=(vmem, vmem),
        scratch_shapes=[
            pltpu.VMEM((id_rows, 128), jnp.int32),
            pltpu.VMEM((1, rows), jnp.int32),
            pltpu.VMEM((part // 128, 128), bf16),
            pltpu.VMEM((vd, rows), bf16),
            pltpu.VMEM((dv, width), bf16),
            pltpu.VMEM((n, rows, part), bf16),
            pltpu.VMEM((rows, width), bf16),
            pltpu.VMEM((vd + 8, rows), f32),
            pltpu.VMEM((slots, rows), f32),
            pltpu.VMEM((n, slots, rows), bf16),
            pltpu.VMEM((n, slots, rows), bf16),
            pltpu.VMEM((n * slots, rows), f32),
            pltpu.VMEM((n * chunks, 128), f32),
            pltpu.VMEM((n * chunks, 128), f32),
            pltpu.VMEM((n * chunks, 128), f32),
            pltpu.VMEM((slot_lanes, 128), f32),
            pltpu.VMEM((n, slot_lanes), jnp.int32),
            pltpu.SMEM((n, slot_lanes), jnp.int32),
            pltpu.VMEM((chunks, 128), jnp.int32),
            pltpu.SMEM((chunks, 128), jnp.int32),
            pltpu.VMEM((dv, rows), f32),
            pltpu.VMEM((dv, rows), f32),
            pltpu.VMEM((dp, rows), f32),
            pltpu.VMEM((rows, dp), bf16),
            pltpu.VMEM((n, 16, 128), f32),
            pltpu.VMEM((side, 8, 128), f32),
            pltpu.VMEM((side, 8, 128), f32),
            pltpu.VMEM((side, 8, 128), f32),
            pltpu.VMEM((side, side, 8, 128), f32),
            pltpu.VMEM((m, 8, 128), f32),
            pltpu.VMEM((8, 128), f32),
            pltpu.VMEM((side, side, rows, part), bf16),
            pltpu.VMEM((side, half, part), f32),
            pltpu.VMEM((side, half, part), f32),
            pltpu.VMEM((side, side, half, part), bf16),
            pltpu.VMEM((side, side, half, part), bf16),
            pltpu.VMEM((side, half, part), bf16),
            pltpu.VMEM((side, half, part), bf16),
            pltpu.VMEM((side, half, part), bf16),
            pltpu.VMEM((side, half, part), bf16),
            dma((8,)),
            pltpu.SemaphoreType.REGULAR,
            pltpu.SemaphoreType.REGULAR,
            dma((side,)),
            dma((side,)),
            dma((side, side)),
            dma((side, side)),
            dma((n,)),
            dma((n,)),
            dma((n,)),
            dma((n,)),
            dma((n,)),
            dma((n,)),
            dma((side,)),
            dma((side,)),
            dma((side,)),
            dma((side,)),
            dma((side,)),
            dma((side,)),
            dma((side,)),
            dma((side,)),
            dma((m,)),
            dma((m,)),
            dma((n,)),
            dma,
            dma((side, side)),
            dma((side, side)),
            dma((side, side)),
            dma((side, side)),
            dma((side,)),
            dma((side,)),
            dma((side,)),
            dma((side,)),
        ],
        compiler_params=pltpu.CompilerParams(
            collective_id=0, has_side_effects=True, vmem_limit_bytes=60 * 1024 * 1024
        ),
    )(
        draft_ids.reshape(id_rows, 128),
        token_ids.reshape(1, rows),
        gain.reshape(part // 128, 128),
        hidden,
        target_logits.T,
        head_weight.T,
    )
    return d_hidden, loss.reshape(rows)


def solution(mesh):
    in_specs = (P("tok", "voc"), P("tok", "voc"), P("voc"), P(None, "voc"), P(), P("tok"))
    out_specs = (P("tok", "voc"), P("tok"))
    return jax.shard_map(
        per_device, mesh=mesh, in_specs=in_specs, out_specs=out_specs, check_vma=False
    )
```

```python
import functools
import math
import jax
import jax.numpy as jnp
from jax import lax
from jax.experimental import pallas as pl
from jax.experimental.pallas import tpu as pltpu
from jax.sharding import PartitionSpec as P

epsilon = 1e-05
MESH = pl.DeviceIdType.MESH
f32 = jnp.float32
bf16 = jnp.bfloat16
NT = (((1,), (1,)), ((), ()))


def up(value, unit):
    return -(-value // unit) * unit


def body(
    dims,
    ids_hbm,
    tok_hbm,
    gain_hbm,
    hid_hbm,
    x_hbm,
    w_hbm,
    dh_ref,
    loss_ref,
    ids_v,
    tok_v,
    gain_v,
    x_v,
    w_v,
    hall,
    nrm,
    table,
    stage,
    psend,
    precv,
    pwide,
    idm_v,
    key_v,
    col_v,
    slot_f,
    slot_v,
    slot_s,
    idx_v,
    idx_s,
    lt,
    pt,
    wide_grad,
    grad,
    stats,
    cross_x,
    cross_y,
    square_x,
    square_y,
    count,
    count_all,
    gsend,
    own_a,
    own_b,
    g1a,
    g1b,
    send_a,
    send_b,
    g2a,
    g2b,
    local_sem,
    entered,
    greeted,
    ha_first,
    hb_first,
    ha_next,
    hb_next,
    ha_recv,
    hb_recv,
    p_send,
    p_recv,
    s_send,
    s_recv,
    qx_send,
    qx_recv,
    qy_send,
    qy_recv,
    tx_send,
    tx_recv,
    ty_send,
    ty_recv,
    c_send,
    c_recv,
    t_send,
    t_recv,
    ga_send,
    gb_send,
    g1a_recv,
    g1b_recv,
    g2a_send,
    g2b_send,
    g2a_recv,
    g2b_recv,
):
    n, m, vd, dv, cap = dims
    side = math.isqrt(n)
    part = hall.shape[2]
    rows = nrm.shape[0]
    half = rows // 2
    width = n * part
    chunks = idx_v.shape[0]
    slots = psend.shape[1]
    i = lax.axis_index("tok")
    j = lax.axis_index("voc")
    x = j // side
    y = lax.rem(j, side)

    def along_x(step):
        return lax.rem(x + step, side)

    def along_y(step):
        return lax.rem(y + step, side)

    copy_ids = pltpu.make_async_copy(ids_hbm, ids_v, local_sem.at[0])
    copy_hid = pltpu.make_async_copy(hid_hbm, hall.at[j, 0:rows], local_sem.at[1])
    copy_gain = pltpu.make_async_copy(gain_hbm, gain_v, local_sem.at[2])
    copy_tok = pltpu.make_async_copy(tok_hbm, tok_v, local_sem.at[3])
    copy_x = pltpu.make_async_copy(x_hbm, x_v, local_sem.at[4])
    copy_w = pltpu.make_async_copy(w_hbm, w_v, local_sem.at[5])
    copy_ids.start()
    copy_hid.start()
    copy_gain.start()
    copy_tok.start()
    copy_x.start()
    copy_w.start()

    barrier = pltpu.get_barrier_semaphore()
    hub = j == 0

    def greet(step, _):
        for peer in (along_x(step) * side + y, x * side + along_y(step)):

            @pl.when(peer != 0)
            def _():
                pl.semaphore_signal(barrier, inc=1, device_id=(i, peer), device_id_type=MESH)

        return 0

    lax.fori_loop(1, side, greet, 0)

    @pl.when(hub)
    def _():
        def greet_tok(step, _):
            peer = lax.rem(i + step, m)
            pl.semaphore_signal(barrier, inc=1, device_id=(peer, j), device_id_type=MESH)
            return 0

        lax.fori_loop(1, m, greet_tok, 0)


    copy_ids.wait()
    lane = lax.broadcasted_iota(jnp.int32, (chunks, 128), 1)
    entry = lax.broadcasted_iota(jnp.int32, (chunks, 128), 0) * 128 + lane
    total_rows = ids_v.shape[0]
    for k in range(n):
        first, shift = divmod(k * dv, 128)
        piece = ids_v[first : min(first + chunks + 1, total_rows), :].astype(f32)
        if shift:
            piece = pltpu.roll(piece, 128 - shift, 1)
        if piece.shape[0] == chunks:
            piece = jnp.concatenate([piece, piece[0:1, :]], axis=0)
        early = jnp.where(lane < 128 - shift, piece[0:chunks, :], piece[1 : chunks + 1, :])
        idm_v[k * chunks : (k + 1) * chunks, :] = jnp.where(entry < dv, early, -1.0)
    ids = idm_v[...]
    low = (j * vd).astype(f32)
    mine = ((ids >= low) & (ids < low + vd)).astype(f32)
    own = idm_v[pl.ds(pl.multiple_of(j * chunks, chunks), chunks), :]
    home = jnp.zeros_like(own)
    for k in range(1, n):
        home += (own >= float(k * vd)).astype(f32)
    home_all = jnp.concatenate([home] * n, axis=0)
    tall = (n * chunks, 128)
    row_shard = (lax.broadcasted_iota(jnp.int32, tall, 0) // chunks).astype(f32)
    hit = (home_all == row_shard).astype(f32)
    before = (
        lax.broadcasted_iota(jnp.int32, (128, 128), 0)
        < lax.broadcasted_iota(jnp.int32, (128, 128), 1)
    ).astype(f32).astype(bf16)
    ones = jnp.ones((128, 128), bf16)
    square_rows = (n * chunks, n * chunks)
    at_row = lax.broadcasted_iota(jnp.int32, square_rows, 0)
    at_column = lax.broadcasted_iota(jnp.int32, square_rows, 1)
    earlier = (
        (at_column < at_row) & (at_column >= at_row - at_row % chunks)
    ).astype(f32).astype(bf16)

    def ranks(mask):
        mask = mask.astype(bf16)
        ahead = jnp.dot(earlier, mask, preferred_element_type=f32).astype(bf16)
        return jnp.dot(mask, before, preferred_element_type=f32) + jnp.dot(
            ahead, ones, preferred_element_type=f32
        )

    key_v[...] = jnp.where(mine > 0.5, ranks(mine), -1.0)
    col_v[...] = ids - low
    rank_hit = ranks(hit) * hit
    rank_own = rank_hit[0:chunks, :]
    for k in range(1, n):
        rank_own += rank_hit[k * chunks : (k + 1) * chunks, :]
    idx_v[...] = jnp.clip((home * slots + rank_own).astype(jnp.int32), 0, n * slots - 1)

    copy_hid.wait()
    copy_gain.wait()
    wide_gain = gain_v[...].astype(f32)
    wide_gain = jnp.concatenate([wide_gain[r : r + 1, :] for r in range(part // 128)], axis=1)

    @pl.when(j != 0)
    def _():
        pl.semaphore_wait(barrier, 2 * (side - 1))

    @pl.when((j != 0) & ((x == 0) | (y == 0)))
    def _():
        pl.semaphore_signal(greeted, inc=1, device_id=(i, 0), device_id_type=MESH)

    @pl.when(hub)
    def _():
        pl.semaphore_wait(greeted, 2 * (side - 1))

    def ha_copy(block, to_x, to_y, send_sem):
        piece = hall.at[block, 0:half]
        return pltpu.make_async_remote_copy(
            src_ref=piece,
            dst_ref=piece,
            send_sem=send_sem,
            recv_sem=ha_recv.at[block],
            device_id=(i, to_x * side + to_y),
            device_id_type=MESH,
        )

    def hb_copy(block, to_x, to_y, send_sem):
        piece = hall.at[block, half:rows]
        return pltpu.make_async_remote_copy(
            src_ref=piece,
            dst_ref=piece,
            send_sem=send_sem,
            recv_sem=hb_recv.at[block],
            device_id=(i, to_x * side + to_y),
            device_id_type=MESH,
        )

    def ha_forward(from_x, step):
        to_y = along_y(step)
        return ha_copy(from_x * side + y, x, to_y, ha_next.at[from_x, to_y])

    def hb_forward(from_y, step):
        to_x = along_x(step)
        return hb_copy(x * side + from_y, to_x, y, hb_next.at[from_y, to_x])

    def h_first(step, _):
        ha_copy(j, along_x(step), y, ha_first.at[along_x(step)]).start()
        hb_copy(j, x, along_y(step), hb_first.at[along_y(step)]).start()
        return 0

    def h_own(step, _):
        ha_forward(x, step).start()
        hb_forward(y, step).start()
        pl.semaphore_signal(
            entered, inc=1, device_id=(i, x * side + along_y(step)), device_id_type=MESH
        )
        return 0

    lax.fori_loop(1, side, h_first, 0)
    lax.fori_loop(1, side, h_own, 0)

    own_hidden = hall[j, 0:rows, :].astype(f32)
    own_squares = jnp.sum(own_hidden * own_hidden, axis=1, keepdims=True)
    square_x[x] = jnp.broadcast_to(own_squares, (rows, 128)).T[0:8, :]
    square_x[x, 1 : 1 + part // 128, :] = gain_v[...].astype(f32)

    def qx_copy(slot, to_x):
        return pltpu.make_async_remote_copy(
            src_ref=square_x.at[slot],
            dst_ref=square_x.at[slot],
            send_sem=qx_send.at[to_x],
            recv_sem=qx_recv.at[slot],
            device_id=(i, to_x * side + y),
            device_id_type=MESH,
        )

    def qy_copy(slot, to_y):
        return pltpu.make_async_remote_copy(
            src_ref=square_y.at[slot],
            dst_ref=square_y.at[slot],
            send_sem=qy_send.at[to_y],
            recv_sem=qy_recv.at[slot],
            device_id=(i, x * side + to_y),
            device_id_type=MESH,
        )

    for step in range(1, side):
        qx_copy(x, along_x(step)).start()

    slot_row = lax.broadcasted_iota(jnp.int32, (slots, 128), 0).astype(f32)
    slot_lane = lax.broadcasted_iota(jnp.int32, (slots, 128), 1)

    def slot_step(k, acc):
        at = pl.multiple_of(k * chunks, chunks)
        keys = key_v[pl.ds(at, chunks), :]
        cols = col_v[pl.ds(at, chunks), :]
        found = jnp.zeros((slots, 128), f32)
        for c in range(chunks):
            found = jnp.where(slot_row == keys[c : c + 1, :], cols[c : c + 1, :] - vd, found)
        return jnp.where(slot_lane == k, jnp.sum(found, axis=1, keepdims=True), acc)

    slot_f[...] = jnp.zeros_like(slot_f)
    slot_f[0:slots, :] = lax.fori_loop(0, n, slot_step, jnp.zeros((slots, 128), f32))
    slot_v[...] = jnp.clip(slot_f[...].T[0:n, :].astype(jnp.int32) + vd, 0, vd)
    copy_slot = pltpu.make_async_copy(slot_v, slot_s, local_sem.at[6])
    copy_idx = pltpu.make_async_copy(idx_v, idx_s, local_sem.at[7])
    copy_slot.start()
    copy_idx.start()

    def h_pass(step, _):
        from_x = along_x(step)
        from_y = along_y(step)
        ha_forward(from_x, 1).wait_recv()
        for later in range(1, side):
            ha_forward(from_x, later).start()
        hb_forward(from_y, 1).wait_recv()
        for later in range(1, side):
            hb_forward(from_y, later).start()
        return 0

    lax.fori_loop(1, side, h_pass, 0)
    for step in range(1, side):
        qx_copy(along_x(step), x).wait_recv()
    square_y[y] = square_x[...]
    for step in range(1, side):
        qy_copy(y, along_y(step)).start()

    copy_tok.wait()
    token_rows = jnp.broadcast_to(tok_v[...].astype(f32), (rows, rows)).T

    def valid_step(k, acc):
        entries = idm_v[pl.ds(pl.multiple_of(k * chunks, chunks), chunks), :]
        for c in range(chunks):
            acc = jnp.where(entries[c : c + 1, :] == token_rows, 1.0, acc)
        return acc

    valid = lax.fori_loop(0, n, valid_step, jnp.zeros((rows, 128), f32))
    valid = jnp.max(valid.T, axis=0, keepdims=True)

    def c_copy(slot, peer):
        return pltpu.make_async_remote_copy(
            src_ref=count.at[i],
            dst_ref=count.at[slot],
            send_sem=c_send.at[peer],
            recv_sem=c_recv.at[slot],
            device_id=(peer, j),
            device_id_type=MESH,
        )

    def t_copy(peer):
        return pltpu.make_async_remote_copy(
            src_ref=count_all,
            dst_ref=count_all,
            send_sem=t_send.at[peer],
            recv_sem=t_recv,
            device_id=(i, peer),
            device_id_type=MESH,
        )

    @pl.when(hub)
    def _():
        pl.semaphore_wait(barrier, m - 1)
        count[i] = jnp.broadcast_to(jnp.sum(valid, axis=1, keepdims=True), (8, 128))

        def c_start(step, _):
            c_copy(i, lax.rem(i + step, m)).start()
            return 0

        lax.fori_loop(1, m, c_start, 0)

    copy_x.wait()
    parts = 3
    span = vd // parts

    def widen_target(c, top):
        at = pl.multiple_of(c * span, 16)
        wide = x_v[pl.ds(at, span), :].astype(f32)
        table[pl.ds(at, span), :] = wide
        return jnp.maximum(top, jnp.max(wide, axis=0, keepdims=True))

    top_target = lax.fori_loop(0, parts, widen_target, jnp.full((1, rows), -1e30, f32))

    copy_slot.wait()
    copy_idx.wait()
    stage[...] = jnp.zeros_like(stage)
    table[vd : vd + 8, :] = jnp.full((8, rows), -1e30, f32)

    def p_copy(slot, peer):
        return pltpu.make_async_remote_copy(
            src_ref=psend.at[peer],
            dst_ref=precv.at[slot],
            send_sem=p_send.at[peer],
            recv_sem=p_recv.at[slot],
            device_id=(i, peer),
            device_id_type=MESH,
        )

    def pick(k):
        for at in range(cap):
            stage[at : at + 1, :] = table[pl.ds(slot_s[k, at], 1), :]
        return stage[...].astype(bf16)

    def pick_mass():
        return jnp.sum(jnp.exp(stage[0:cap, :] - top_target), axis=0, keepdims=True)

    def pick_step(step, acc):
        peer = lax.rem(j + step, n)
        psend[peer] = pick(peer)
        return acc + pick_mass()

    mass_here = lax.fori_loop(1, n, pick_step, jnp.zeros((1, rows), f32))
    precv[j] = pick(j)
    mass_here += pick_mass()

    total_target = lax.fori_loop(
        0,
        parts,
        lambda c, total: total
        + jnp.sum(
            jnp.exp(table[pl.ds(pl.multiple_of(c * span, 8), span), :] - top_target),
            axis=0,
            keepdims=True,
        ),
        jnp.zeros((1, rows), f32),
    )

    for step in range(1, side):
        qy_copy(along_y(step), y).wait_recv()
    squares = jnp.sum(jnp.sum(square_y[...], axis=0), axis=0)[0:1, :]
    inv_row = lax.rsqrt(squares / width + epsilon)
    inv = jnp.broadcast_to(inv_row, (rows, rows)).T[:, 0:1]

    def p_start(step, _):
        p_copy(j, lax.rem(j + step, n)).start()
        return 0

    def normalise(xs, ys):
        k = xs * side + ys
        wide = hall[k, 0:rows, :].astype(f32)
        tile = square_y[ys, xs]
        gains = jnp.concatenate([tile[r + 1 : r + 2, :] for r in range(part // 128)], axis=1)
        at = pl.multiple_of(k * part, part)
        nrm[:, pl.ds(at, part)] = (wide * inv * gains).astype(bf16)

    for step in range(side):
        from_x = along_x(step)
        for other in range(1, side):
            from_y = along_y(other)
            ha_copy(from_x * side + from_y, x, from_y, ha_next.at[0, 0]).wait_recv()
        if step:
            for other in range(side):
                hb_copy(from_x * side + other, from_x, y, hb_next.at[0, 0]).wait_recv()
        if step == 0:
            pl.semaphore_wait(entered, side - 1)
            lax.fori_loop(1, n, p_start, 0)
        for other in range(side):
            normalise(from_x, other)
        if step == 0:
            copy_w.wait()
        at = pl.ds(pl.multiple_of(from_x * side * part, part), side * part)
        share = lax.dot_general(w_v[:, at], nrm[:, at], NT, preferred_element_type=f32)
        if step:
            lt[...] += share
        else:
            lt[...] = share

    draft = lt[...]
    top_draft = jnp.max(draft, axis=0, keepdims=True)
    lifted = jnp.exp(draft - top_draft)
    total_draft = jnp.sum(lifted, axis=0, keepdims=True)
    cross_draft = jnp.sum(lifted * draft, axis=0, keepdims=True)

    tops = (top_target, top_target, top_draft, top_draft)
    sums = (total_target, mass_here, total_draft, cross_draft)
    stats[j] = jnp.zeros((16, 128), f32)
    for r in range(4):
        stats[j, r : r + 1, :] = tops[r]
        stats[j, 8 + r : 9 + r, :] = sums[r]

    @pl.when(hub)
    def _():
        def c_wait(step, _):
            c_copy(lax.rem(i + step, m), i).wait_recv()
            return 0

        lax.fori_loop(1, m, c_wait, 0)
        count_all[...] = jnp.sum(count[...], axis=0)

        def t_start(peer, _):
            t_copy(peer).start()
            return 0

        lax.fori_loop(1, n, t_start, 0)

    def s_copy(slot, peer):
        return pltpu.make_async_remote_copy(
            src_ref=stats.at[slot],
            dst_ref=stats.at[slot],
            send_sem=s_send.at[peer],
            recv_sem=s_recv.at[slot],
            device_id=(i, peer),
            device_id_type=MESH,
        )

    def merge(ref):
        top = ref[0, 0:8, :]
        for k in range(1, n):
            top = jnp.maximum(top, ref[k, 0:8, :])
        total = jnp.zeros((8, 128), f32)
        for k in range(n):
            total += ref[k, 8:16, :] * jnp.exp(ref[k, 0:8, :] - top)
        return top, total

    def s_start(step, _):
        s_copy(j, lax.rem(j + step, n)).start()
        return 0

    def s_wait(step, _):
        s_copy(lax.rem(j + step, n), j).wait_recv()
        return 0

    lax.fori_loop(1, n, s_start, 0)
    lax.fori_loop(1, n, s_wait, 0)
    top, total = merge(stats)

    target_lse = top[0:1, :] + jnp.log(total[0:1, :])
    mass = total[1:2, :] * jnp.exp(top[1:2, :] - target_lse)
    draft_lse = top[2:3, :] + jnp.log(total[2:3, :])
    mean_draft = total[3:4, :] / total[2:3, :]
    wide_grad[dv:, :] = jnp.zeros((wide_grad.shape[0] - dv, rows), f32)
    wide_grad[0:dv, :] = mass * jnp.exp(lt[...] - draft_lse)

    def widen(k):
        pwide[pl.ds(pl.multiple_of(k * slots, 8), slots), :] = precv[k].astype(f32)

    def p_wait(step, _):
        slot = lax.rem(j + step, n)
        p_copy(slot, j).wait_recv()
        widen(slot)
        return 0

    widen(j)
    lax.fori_loop(1, n, p_wait, 0)
    for at in range(dv):
        pt[at : at + 1, :] = pwide[pl.ds(idx_s[at // 128, at % 128], 1), :]
    @pl.when(j != 0)
    def _():
        t_copy(0).wait_recv()

    weight = valid * (float(rows * m) / count_all[0:1, :])
    probs = jnp.exp(pt[...] - target_lse)
    wide_grad[0:dv, :] = weight * (wide_grad[0:dv, :] - probs)
    grad[...] = wide_grad[...].T.astype(bf16)

    def term(to_x, to_y):
        at = pl.multiple_of((to_x * side + to_y) * part, part)
        return jnp.dot(grad[:, 0:dv], w_v[:, pl.ds(at, part)], preferred_element_type=f32)

    def g1a_copy(from_x, to_x, to_y):
        return pltpu.make_async_remote_copy(
            src_ref=gsend.at[to_x, to_y, 0:half],
            dst_ref=g1a.at[from_x, to_y],
            send_sem=ga_send.at[to_x, to_y],
            recv_sem=g1a_recv.at[from_x, to_y],
            device_id=(i, to_x * side + y),
            device_id_type=MESH,
        )

    def g1b_copy(from_y, to_x, to_y):
        return pltpu.make_async_remote_copy(
            src_ref=gsend.at[to_x, to_y, half:rows],
            dst_ref=g1b.at[from_y, to_x],
            send_sem=gb_send.at[to_x, to_y],
            recv_sem=g1b_recv.at[from_y, to_x],
            device_id=(i, x * side + to_y),
            device_id_type=MESH,
        )

    def g_both(t, _):
        to_x = along_x(t // (side - 1) + 1)
        to_y = along_y(t % (side - 1) + 1)
        gsend[to_x, to_y] = term(to_x, to_y).astype(bf16)
        g1a_copy(x, to_x, to_y).start()
        g1b_copy(y, to_x, to_y).start()
        return 0

    def g_column(step, _):
        to_x = along_x(step)
        value = term(to_x, y)
        gsend[to_x, y] = value.astype(bf16)
        g1a_copy(x, to_x, y).start()
        own_b[to_x] = value[half:rows, :]
        return 0

    def g_row(step, _):
        to_y = along_y(step)
        value = term(x, to_y)
        gsend[x, to_y] = value.astype(bf16)
        g1b_copy(y, x, to_y).start()
        own_a[to_y] = value[0:half, :]
        return 0

    lax.fori_loop(0, (side - 1) * (side - 1), g_both, 0)
    cross_x[x] = jnp.broadcast_to(jnp.sum(jnp.exp(pt[...] - target_lse) * lt[...], axis=0, keepdims=True), (8, rows))

    def tx_copy(slot, to_x):
        return pltpu.make_async_remote_copy(
            src_ref=cross_x.at[slot],
            dst_ref=cross_x.at[slot],
            send_sem=tx_send.at[to_x],
            recv_sem=tx_recv.at[slot],
            device_id=(i, to_x * side + y),
            device_id_type=MESH,
        )

    def ty_copy(slot, to_y):
        return pltpu.make_async_remote_copy(
            src_ref=cross_y.at[slot],
            dst_ref=cross_y.at[slot],
            send_sem=ty_send.at[to_y],
            recv_sem=ty_recv.at[slot],
            device_id=(i, x * side + to_y),
            device_id_type=MESH,
        )

    for step in range(1, side):
        tx_copy(x, along_x(step)).start()

    lax.fori_loop(1, side, g_column, 0)
    lax.fori_loop(1, side, g_row, 0)
    value = term(x, y)
    own_a[y] = value[0:half, :]
    own_b[x] = value[half:rows, :]

    for step in range(1, side):
        tx_copy(along_x(step), x).wait_recv()
    cross_y[y] = jnp.sum(cross_x[...], axis=0)
    for step in range(1, side):
        ty_copy(y, along_y(step)).start()

    def sum_a(to_y):
        acc = own_a[to_y]
        for step in range(1, side):
            from_x = along_x(step)
            g1a_copy(from_x, x, to_y).wait_recv()
            acc += g1a[from_x, to_y].astype(f32)
        return acc

    def sum_b(to_x):
        acc = own_b[to_x]
        for step in range(1, side):
            from_y = along_y(step)
            g1b_copy(from_y, to_x, y).wait_recv()
            acc += g1b[from_y, to_x].astype(f32)
        return acc

    def g2a_copy(from_y, to_y):
        return pltpu.make_async_remote_copy(
            src_ref=send_a.at[to_y],
            dst_ref=g2a.at[from_y],
            send_sem=g2a_send.at[to_y],
            recv_sem=g2a_recv.at[from_y],
            device_id=(i, x * side + to_y),
            device_id_type=MESH,
        )

    def g2b_copy(from_x, to_x):
        return pltpu.make_async_remote_copy(
            src_ref=send_b.at[to_x],
            dst_ref=g2b.at[from_x],
            send_sem=g2b_send.at[to_x],
            recv_sem=g2b_recv.at[from_x],
            device_id=(i, to_x * side + y),
            device_id_type=MESH,
        )

    def g_second(step, _):
        to_y = along_y(step)
        send_a[to_y] = sum_a(to_y).astype(bf16)
        g2a_copy(y, to_y).start()
        to_x = along_x(step)
        send_b[to_x] = sum_b(to_x).astype(bf16)
        g2b_copy(x, to_x).start()
        return 0

    lax.fori_loop(1, side, g_second, 0)
    for step in range(1, side):
        ty_copy(along_y(step), y).wait_recv()
    cross = jnp.sum(cross_y[...], axis=0)[0:1, :]
    loss_ref[...] = weight * (mass * draft_lse - cross)
    spread = weight * (mass * mean_draft - cross)
    shrink = inv_row * inv_row * spread / width
    shrink = jnp.broadcast_to(shrink, (rows, rows)).T[:, 0:1]
    first = sum_a(y)
    second = sum_b(x)
    for step in range(1, side):
        from_y = along_y(step)
        g2a_copy(from_y, y).wait_recv()
        first += g2a[from_y].astype(f32)
        from_x = along_x(step)
        g2b_copy(from_x, x).wait_recv()
        second += g2b[from_x].astype(f32)
    wide_hidden = hall[j, 0:rows, :].astype(f32)
    dh_ref[0:half, :] = (
        wide_gain * inv[0:half, :] * first - wide_hidden[0:half, :] * shrink[0:half, :]
    )
    dh_ref[half:rows, :] = (
        wide_gain * inv[half:rows, :] * second - wide_hidden[half:rows, :] * shrink[half:rows, :]
    )

    def finish_voc(step, _):
        peer = lax.rem(j + step, n)
        p_copy(j, peer).wait_send()
        s_copy(j, peer).wait_send()
        return 0

    def finish_side(step, _):
        to_x = along_x(step)
        to_y = along_y(step)
        ha_copy(j, to_x, y, ha_first.at[to_x]).wait_send()
        hb_copy(j, x, to_y, hb_first.at[to_y]).wait_send()
        for origin in range(side):
            ha_forward(origin, step).wait_send()
            hb_forward(origin, step).wait_send()
        qx_copy(x, to_x).wait_send()
        qy_copy(y, to_y).wait_send()
        tx_copy(x, to_x).wait_send()
        ty_copy(y, to_y).wait_send()
        for other in range(side):
            g1a_copy(x, to_x, other).wait_send()
            g1b_copy(y, other, to_y).wait_send()
        g2a_copy(y, to_y).wait_send()
        g2b_copy(x, to_x).wait_send()
        return 0

    lax.fori_loop(1, n, finish_voc, 0)
    lax.fori_loop(1, side, finish_side, 0)

    @pl.when(hub)
    def _():
        def finish_tok(step, _):
            c_copy(i, lax.rem(i + step, m)).wait_send()
            return 0

        def finish_total(peer, _):
            t_copy(peer).wait_send()
            return 0

        lax.fori_loop(1, m, finish_tok, 0)
        lax.fori_loop(1, n, finish_total, 0)


def per_device(target_logits, hidden, gain, head_weight, draft_ids, token_ids):
    n = lax.axis_size("voc")
    m = lax.axis_size("tok")
    rows, part = hidden.shape
    vd = target_logits.shape[1]
    width, dv = head_weight.shape
    side = math.isqrt(n)
    half = rows // 2
    cap = 8 * (5 * dv // (16 * n))
    slots = up(cap, 16)
    dp = up(dv, 128)
    chunks = dp // 128
    slot_lanes = up(slots, 128)
    id_rows = n * dv // 128
    vmem = pl.BlockSpec(memory_space=pltpu.VMEM)
    anywhere = pl.BlockSpec(memory_space=pl.ANY)
    dma = pltpu.SemaphoreType.DMA
    d_hidden, loss = pl.pallas_call(
        functools.partial(body, (n, m, vd, dv, cap)),
        out_shape=(
            jax.ShapeDtypeStruct((rows, part), f32),
            jax.ShapeDtypeStruct((1, rows), f32),
        ),
        in_specs=[anywhere] * 6,
        out_specs=(vmem, vmem),
        scratch_shapes=[
            pltpu.VMEM((id_rows, 128), jnp.int32),
            pltpu.VMEM((1, rows), jnp.int32),
            pltpu.VMEM((part // 128, 128), bf16),
            pltpu.VMEM((vd, rows), bf16),
            pltpu.VMEM((dv, width), bf16),
            pltpu.VMEM((n, rows, part), bf16),
            pltpu.VMEM((rows, width), bf16),
            pltpu.VMEM((vd + 8, rows), f32),
            pltpu.VMEM((slots, rows), f32),
            pltpu.VMEM((n, slots, rows), bf16),
            pltpu.VMEM((n, slots, rows), bf16),
            pltpu.VMEM((n * slots, rows), f32),
            pltpu.VMEM((n * chunks, 128), f32),
            pltpu.VMEM((n * chunks, 128), f32),
            pltpu.VMEM((n * chunks, 128), f32),
            pltpu.VMEM((slot_lanes, 128), f32),
            pltpu.VMEM((n, slot_lanes), jnp.int32),
            pltpu.SMEM((n, slot_lanes), jnp.int32),
            pltpu.VMEM((chunks, 128), jnp.int32),
            pltpu.SMEM((chunks, 128), jnp.int32),
            pltpu.VMEM((dv, rows), f32),
            pltpu.VMEM((dv, rows), f32),
            pltpu.VMEM((dp, rows), f32),
            pltpu.VMEM((rows, dp), bf16),
            pltpu.VMEM((n, 16, 128), f32),
            pltpu.VMEM((side, 8, 128), f32),
            pltpu.VMEM((side, 8, 128), f32),
            pltpu.VMEM((side, 8, 128), f32),
            pltpu.VMEM((side, side, 8, 128), f32),
            pltpu.VMEM((m, 8, 128), f32),
            pltpu.VMEM((8, 128), f32),
            pltpu.VMEM((side, side, rows, part), bf16),
            pltpu.VMEM((side, half, part), f32),
            pltpu.VMEM((side, half, part), f32),
            pltpu.VMEM((side, side, half, part), bf16),
            pltpu.VMEM((side, side, half, part), bf16),
            pltpu.VMEM((side, half, part), bf16),
            pltpu.VMEM((side, half, part), bf16),
            pltpu.VMEM((side, half, part), bf16),
            pltpu.VMEM((side, half, part), bf16),
            dma((8,)),
            pltpu.SemaphoreType.REGULAR,
            pltpu.SemaphoreType.REGULAR,
            dma((side,)),
            dma((side,)),
            dma((side, side)),
            dma((side, side)),
            dma((n,)),
            dma((n,)),
            dma((n,)),
            dma((n,)),
            dma((n,)),
            dma((n,)),
            dma((side,)),
            dma((side,)),
            dma((side,)),
            dma((side,)),
            dma((side,)),
            dma((side,)),
            dma((side,)),
            dma((side,)),
            dma((m,)),
            dma((m,)),
            dma((n,)),
            dma,
            dma((side, side)),
            dma((side, side)),
            dma((side, side)),
            dma((side, side)),
            dma((side,)),
            dma((side,)),
            dma((side,)),
            dma((side,)),
        ],
        compiler_params=pltpu.CompilerParams(
            collective_id=0, has_side_effects=True, vmem_limit_bytes=60 * 1024 * 1024
        ),
    )(
        draft_ids.reshape(id_rows, 128),
        token_ids.reshape(1, rows),
        gain.reshape(part // 128, 128),
        hidden,
        target_logits.T,
        head_weight.T,
    )
    return d_hidden, loss.reshape(rows)


def solution(mesh):
    in_specs = (P("tok", "voc"), P("tok", "voc"), P("voc"), P(None, "voc"), P(), P("tok"))
    out_specs = (P("tok", "voc"), P("tok"))
    return jax.shard_map(
        per_device, mesh=mesh, in_specs=in_specs, out_specs=out_specs, check_vma=False
    )
```
